256 devices in a mesh: dp: 8 (over z_lo, core), ctx: 32 (over x, z_hi, y).
Axes of the slice: x: 4, y: 4, z: 8 (z_hi: 2, z_lo: 4; z = z_hi * 4 + z_lo), core: 2. Of those that a mesh axis runs over, the one named last changes fastest.
Arguments:
- queries: bfloat16 [8, 4096, 12288], P('dp', 'ctx'), may hold values from -6 to 115
- grad_out: bfloat16 [8, 4096, 8192], P('dp', 'ctx'), may hold values from -6 to 6
- latent: bfloat16 [8, 4096, 576], P('dp', 'ctx'), may hold values from -6 to 6
- up_weight: bfloat16 [512, 16384], P(None, 'ctx'), may hold values from -0.25 to 0.25
- doc_lengths: int32 [8, 128], P('dp'), may hold values from 1 to 64, 4096 in all within a row
- stretch_order: int32 [8, 64], P('dp'), may hold values from 0 to 63, each once within a row
Outputs:
- grad_queries: bfloat16 [8, 4096, 12288], P('dp', 'ctx')
- grad_latent: bfloat16 [8, 4096, 576], P('dp', 'ctx')
- grad_weight: float32 [512, 16384], P(None, 'ctx')
The draws below stay inside these ranges and needn't reach their ends.
Inputs may be any that keep to these rules, and one draw needn't show every extreme that they name: `doc_lengths`: each row sums to 4096 and its largest length is exactly 64. `stretch_order`: each row names every block once.
All inputs are finite; a program needn't handle non-finite values.
Results may differ from the reference program's by a relative error of at most 0.03.
Values may be sent and summed in bfloat16 or wider, within the bound.
A program may use at most 128 MiB of HBM per device.

```python
import math
import jax
import jax.numpy as jnp
import numpy as np
from jax import lax

HEADS = 64
D_NOPE = 128
D_ROPE = 64
D_V = 128
D_LAT = 512
QB = 512
STRETCH = 64
DOC_MOST = 64
TOKENS = 4096
NDOC = 128
BATCH = 8
HEADS_DEV = 2
N_CTX = 32


def draw_queries(key, part):
    key = jax.random.fold_in(key, 11)
    shape = (BATCH, TOKENS, HEADS, D_NOPE + D_ROPE)
    base = jnp.clip(jax.random.normal(key, shape, jnp.float32), -6.0, 6.0)
    return base.reshape(BATCH, TOKENS, HEADS * (D_NOPE + D_ROPE)).astype(jnp.bfloat16)


def draw_latent(key, part):
    key = jax.random.fold_in(key, 13)
    shape = (BATCH, TOKENS, D_LAT + D_ROPE)
    base = jnp.clip(jax.random.normal(key, shape, jnp.float32), -6.0, 6.0)
    return base.astype(jnp.bfloat16)


def block_scale(stream_key, dims, split, low, largest):
    loudness = 1.0
    for dim, blocks in split:
        heights = jax.random.uniform(jax.random.fold_in(jax.random.fold_in(stream_key, 6), dim), (blocks,), jnp.float32, low / len(split), largest / len(split))
        loudness = loudness * jnp.repeat(jnp.exp(heights), dims[dim] // blocks).reshape((-1,) + (1,) * (len(dims) - 1 - dim))
    return loudness


def length_profile(amount, total, limit, slope):
    weights = [(1 << 20) // math.isqrt(standing ** slope) + 1 for standing in range(2, amount + 1)]
    rest, counts = total - limit - (amount - 1), [1] * (amount - 1)
    while rest > 0:
        candidates = [i for i in range(amount - 1) if counts[i] < limit]
        pool, budget = sum([weights[i] for i in candidates]), rest
        for i in candidates:
            addition = min(limit - counts[i], max(1, budget * weights[i] // pool), rest)
            counts[i] = counts[i] + addition
            rest = rest - addition
    return np.array([limit] + counts)


def uneven_parts(own_key, count, total, most, skew):
    if count == 2:
        one = jax.random.randint(own_key, (), max(1, total - most), min(most, total - 1) + 1)
        return jnp.stack([one, total - one])
    tallies = jnp.asarray(length_profile(count, total, most, skew), jnp.int32)
    twos = (count - 1) // 2
    source_of, taker = tallies[1:1 + 2 * twos:2], tallies[2:2 + 2 * twos:2]
    room = jnp.minimum(source_of - 1, most - taker)
    moved = jax.random.randint(jax.random.fold_in(own_key, 1), (twos,), 0, 1 << 20) % (room + 1)
    tallies = tallies.at[1:1 + 2 * twos:2].set(source_of - moved).at[2:2 + 2 * twos:2].set(taker + moved)
    return tallies[jax.random.permutation(jax.random.fold_in(own_key, 2), count)]


def gaussian(key, dims, scale, limit, split=(), kind=jnp.bfloat16):
    result = jax.random.normal(key, dims, jnp.float32) * scale
    if len(split) > 0:
        result = block_scale(key, dims, split, -0.22, 0.18) * result
    return jnp.clip(result, min=-limit, max=limit).astype(kind)


def setup_inputs(seed: int = 0) -> dict:
    seeds = jax.random.split(jax.random.key(seed), 7)
    queries = draw_queries(jax.random.fold_in(seeds[6], 71), 0)
    grad_out = gaussian(seeds[1], (BATCH, TOKENS, HEADS * D_V), 1.0, 6.0, ((0, 8), (1, 32)))
    latent = draw_latent(jax.random.fold_in(seeds[6], 71), 0)
    up_weight = gaussian(seeds[3], (D_LAT, HEADS * (D_NOPE + D_V)), D_LAT ** -0.5, 0.25, ((1, 32),))
    doc_lengths = jax.vmap(lambda own: uneven_parts(own, NDOC, TOKENS, DOC_MOST, 1))(jax.random.split(seeds[4], BATCH)).reshape((BATCH, NDOC)).astype(jnp.int32)
    stretch_order = jax.vmap(lambda own: jax.random.permutation(own, 2 * N_CTX))(jax.random.split(seeds[5], BATCH)).reshape((BATCH, 2 * N_CTX)).astype(jnp.int32)
    return {"queries": queries, "grad_out": grad_out, "latent": latent, "up_weight": up_weight, "doc_lengths": doc_lengths, "stretch_order": stretch_order}


def pad_front(array, behind, filler):
    front_rows = jnp.full((behind,) + array.shape[1:], filler, array.dtype)
    return jnp.concatenate([front_rows, array], 0)


def fold_windows(windows, behind):
    front_part = windows[:, :behind]
    main_part = windows[:, behind:]
    carried = jnp.concatenate([front_part[1:], jnp.zeros_like(front_part[:1])], 0)
    main_part = main_part.at[:, QB - behind:].add(carried)
    return main_part.reshape((-1,) + main_part.shape[2:])


def rounded(array):
    return lax.optimization_barrier(array.astype(jnp.bfloat16)).astype(jnp.float32)


def banded(query_all, grad_all, keys_nope, values, keys_rope, doc_ids):
    tokens_all = query_all.shape[0]
    behind = DOC_MOST
    scale = (D_NOPE + D_ROPE) ** -0.5
    positions = jnp.arange(tokens_all, dtype=jnp.int32)
    keys_pad = pad_front(keys_nope, behind, 0)
    values_pad = pad_front(values, behind, 0)
    rotary_pad = pad_front(keys_rope, behind, 0)
    key_pos = pad_front(positions, behind, -1)
    key_doc = pad_front(doc_ids, behind, -1)

    def one_block(index):
        row_start = index * QB
        span = QB + behind
        query_blk = lax.dynamic_slice_in_dim(query_all, row_start, QB, 0).astype(jnp.float32)
        grad_blk = lax.dynamic_slice_in_dim(grad_all, row_start, QB, 0).astype(jnp.float32)
        key_blk = lax.dynamic_slice_in_dim(keys_pad, row_start, span, 0).astype(jnp.float32)
        value_blk = lax.dynamic_slice_in_dim(values_pad, row_start, span, 0).astype(jnp.float32)
        rotary_blk = lax.dynamic_slice_in_dim(rotary_pad, row_start, span, 0).astype(jnp.float32)
        pos_blk = lax.dynamic_slice_in_dim(key_pos, row_start, span, 0)
        doc_blk = lax.dynamic_slice_in_dim(key_doc, row_start, span, 0)
        query_pos = row_start + jnp.arange(QB, dtype=jnp.int32)
        query_doc = lax.dynamic_slice_in_dim(doc_ids, row_start, QB, 0)
        allowed = (pos_blk[None, :] <= query_pos[:, None]) & (doc_blk[None, :] == query_doc[:, None])
        query_nope = query_blk[..., :D_NOPE]
        query_rope = query_blk[..., D_NOPE:]
        scores = (jnp.einsum("qhd,khd->hqk", query_nope, key_blk) + jnp.einsum("qhd,kd->hqk", query_rope, rotary_blk)) * scale
        scores = jnp.where(allowed[None], scores, -jnp.inf)
        highest = jnp.max(scores, -1, keepdims=True)
        expo = jnp.exp(scores - highest)
        probs = expo / jnp.sum(expo, -1, keepdims=True)
        dprob = jnp.einsum("qhd,khd->hqk", grad_blk, value_blk)
        delta = jnp.sum(probs * dprob, -1, keepdims=True)
        dscore = rounded(probs * (dprob - delta) * scale)
        probs_low = rounded(probs)
        grad_nope = jnp.einsum("hqk,khd->qhd", dscore, key_blk)
        grad_rope = jnp.einsum("hqk,kd->qhd", dscore, rotary_blk)
        grad_query = jnp.concatenate([grad_nope, grad_rope], -1).astype(jnp.bfloat16)
        grad_values = jnp.einsum("hqk,qhd->khd", probs_low, grad_blk)
        grad_keys = jnp.einsum("hqk,qhd->khd", dscore, query_nope)
        grad_rotary = jnp.einsum("hqk,qhd->khd", dscore, query_rope)
        return grad_query, grad_keys, grad_values, grad_rotary

    results = lax.map(one_block, jnp.arange(tokens_all // QB, dtype=jnp.int32))
    grad_query = results[0].reshape((tokens_all,) + results[0].shape[2:])
    return grad_query, fold_windows(results[1], behind), fold_windows(results[2], behind), fold_windows(results[3], behind)


def reference(queries, grad_out, latent, up_weight, doc_lengths, stretch_order):
    head_cols = D_NOPE + D_V
    width = HEADS_DEV * head_cols
    weight_total = jnp.zeros((D_LAT, HEADS * head_cols), jnp.float32)
    query_list = []
    latent_list = []
    for trace in range(BATCH):
        storage_order = stretch_order[trace].astype(jnp.int32)
        inverse = jnp.argsort(storage_order).astype(jnp.int32)

        def to_natural(array):
            blocks = array.reshape((2 * N_CTX, STRETCH) + array.shape[1:])
            return jnp.take(blocks, inverse, axis=0).reshape(array.shape)

        def to_storage(array):
            blocks = array.reshape((2 * N_CTX, STRETCH) + array.shape[1:])
            return jnp.take(blocks, storage_order, axis=0).reshape(array.shape)

        ends = jnp.cumsum(doc_lengths[trace]).astype(jnp.int32)
        positions = jnp.arange(TOKENS, dtype=jnp.int32)
        doc_ids = jnp.sum((ends[None, :] <= positions[:, None]).astype(jnp.int32), 1).astype(jnp.int32)
        latent_nat = to_natural(latent[trace])
        query_nat = to_natural(queries[trace]).reshape(TOKENS, HEADS, D_NOPE + D_ROPE)
        grad_nat = to_natural(grad_out[trace]).reshape(TOKENS, HEADS, D_V)
        keys_values = jnp.dot(latent_nat[:, :D_LAT], up_weight, preferred_element_type=jnp.float32).astype(jnp.bfloat16)
        keys_values = keys_values.reshape(TOKENS, HEADS, head_cols)
        grad_query, grad_keys, grad_values, grad_rotary = banded(query_nat, grad_nat, keys_values[..., :D_NOPE], keys_values[..., D_NOPE:], latent_nat[:, D_LAT:], doc_ids)
        grad_kv = jnp.concatenate([grad_keys, grad_values], -1).astype(jnp.bfloat16).reshape(TOKENS, HEADS * head_cols)
        weight_total = weight_total + lax.dot_general(latent_nat[:, :D_LAT], grad_kv, (((0,), (0,)), ((), ())), preferred_element_type=jnp.float32)
        latent_total = jnp.zeros((TOKENS, D_LAT + D_ROPE), jnp.float32)
        for group in range(N_CTX):
            cols_kv = grad_kv[:, group * width:(group + 1) * width]
            cols_w = up_weight[:, group * width:(group + 1) * width]
            lat_part = lax.dot_general(cols_kv, cols_w, (((1,), (1,)), ((), ())), preferred_element_type=jnp.float32)
            rope_part = jnp.sum(grad_rotary[:, group * HEADS_DEV:(group + 1) * HEADS_DEV], 1)
            latent_total = latent_total + rounded(jnp.concatenate([lat_part, rope_part], 1))
        query_list.append(to_storage(grad_query.reshape(TOKENS, HEADS * (D_NOPE + D_ROPE))))
        latent_list.append(to_storage(latent_total.astype(jnp.bfloat16)))
    return jnp.stack(query_list), jnp.stack(latent_list), weight_total
```

```python
import jax
import jax.numpy as jnp
from jax import lax
from jax.experimental import pallas as pl
from jax.experimental.pallas import tpu as pltpu
from jax.sharding import PartitionSpec as P


BF16 = jnp.bfloat16
F32 = jnp.float32
MESH = pl.DeviceIdType.MESH

D_NOPE = 128
D_ROPE = 64
D_V = 128
D_LAT = 512
D_ALL = D_LAT + D_ROPE
STRETCH = 64
OWN = 128
KEYS = 256
QW = 2 * (D_NOPE + D_ROPE)
VW = 2 * D_V
KVW = 2 * (D_NOPE + D_V)
SCALE = (D_NOPE + D_ROPE) ** -0.5
HALF = D_LAT // 2
QUARTER = D_LAT // 4
VMEM_LIMIT = 60 * 1024 * 1024


def gray(index):
    return index + index // 2 - 2 * (index // 3)


GRAY = [0, 1, 3, 2]
UNGRAY = [0, 1, 3, 2]


def slot_of(dx, dy):
    return 4 * UNGRAY[dy % 4] + UNGRAY[dx % 4]


def rows_of(half, piece):
    base = half * HALF
    if piece == "f":
        return base, HALF
    return base + int(piece) * QUARTER, QUARTER


def main_axis(half):
    return "x" if half == 0 else "y"


def at(axis, along, across):
    return (along, across) if axis == "x" else (across, along)


class Coords:
    def __init__(self):
        dp, ctx = lax.axis_index("dp"), lax.axis_index("ctx")
        self.dp, self.ctx = dp, ctx
        self.zl, self.core = dp // 2, dp % 2
        self.x, self.zh, self.y = ctx // 8, (ctx // 4) % 2, ctx % 4

    def device(self, x=None, y=None, zh=None, zl=None, core=None):
        x = self.x if x is None else x
        y = self.y if y is None else y
        zh = self.zh if zh is None else zh
        zl = self.zl if zl is None else zl
        core = self.core if core is None else core
        return (zl * 2 + core, (x * 2 + zh) * 4 + y)

    def neighbour(self, axis, sign):
        if axis == "x":
            return self.device(x=(self.x + 4 + sign) % 4)
        return self.device(y=(self.y + 4 + sign) % 4)


def gather_keys():
    keys = []
    for half in (0, 1):
        axis = main_axis(half)
        for across in range(4):
            for along in range(4):
                dx, dy = at(axis, along, across)
                if along == 0 and across == 0:
                    continue
                last = across if across else along
                for piece in ("0", "1") if last == 2 else ("f",):
                    keys.append((half, dx, dy, piece))
    return {key: i for i, key in enumerate(keys)}


GATHER = gather_keys()


def reduce_keys():
    keys, row = {}, 0
    for half in (0, 1):
        for across in range(4):
            for phase in (0, 1):
                if phase == 1 and across:
                    continue
                for piece, count in (("0", QUARTER), ("1", QUARTER), ("from1", HALF), ("from3", HALF)):
                    keys[(half, phase, across, piece)] = (len(keys), row, count)
                    row += count
    return keys, row


REDUCE, REDUCE_ROWS = reduce_keys()


def main_kernel(
    q_hbm,
    go_hbm,
    lat_ref,
    klo_ref,
    w_ref,
    gq_hbm,
    glat_ref,
    sum_ref,
    qbuf,
    gobuf,
    gqbuf,
    latb,
    lat_t,
    klob,
    bias,
    wbuf,
    gbuf,
    rbuf,
    kvbuf,
    gkvbuf,
    acc,
    accin,
    loc_q,
    loc_go,
    rem_q,
    rem_go,
    snd_q,
    snd_go,
    misc,
    wz,
    ag_send,
    ag_recv,
    rs_send,
    rs_recv,
    gq_loc,
    gq_snd,
    gq_rcv,
):
    me = Coords()
    core, other = me.core, 1 - me.core
    partner = me.device(core=other)
    is_source = me.zh == core
    up = me.zl >= 2
    sends_up = jnp.logical_and(is_source, me.zl == 3)
    sends_down = jnp.logical_and(is_source, me.zl == 0)
    z_source = me.device(zh=1 - me.zh, zl=jnp.where(up, 0, 3))

    barrier = pltpu.get_barrier_semaphore()
    for device in (
        me.neighbour("x", 1),
        me.neighbour("x", -1),
        me.neighbour("y", 1),
        me.neighbour("y", -1),
        partner,
    ):
        pl.semaphore_signal(barrier, inc=1, device_id=device, device_id_type=MESH)

    @pl.when(jnp.logical_not(is_source))
    def _():
        pl.semaphore_signal(barrier, inc=1, device_id=z_source, device_id_type=MESH)

    pl.semaphore_wait(barrier, 5 + 2 * jnp.logical_or(sends_up, sends_down).astype(jnp.int32))

    def z_copy(zl, half):
        return pltpu.make_async_remote_copy(
            src_ref=w_ref.at[pl.ds(half * HALF, HALF)],
            dst_ref=wbuf.at[0, pl.ds(half * HALF, HALF)],
            send_sem=wz.at[half + 2 * (0 if zl in (0, 3) else 1)],
            recv_sem=wz.at[4 + half],
            device_id=me.device(zh=1 - me.zh, zl=zl),
            device_id_type=MESH,
        )

    @pl.when(sends_up)
    def _():
        for half in (0, 1):
            for zl in (0, 1):
                z_copy(zl, half).start()

    @pl.when(sends_down)
    def _():
        for half in (0, 1):
            for zl in (3, 2):
                z_copy(zl, half).start()

    lat_own = pltpu.make_async_copy(lat_ref, latb.at[core], misc.at[0])
    lat_own.start()
    klo_own = pltpu.make_async_copy(klo_ref, klob.at[core], misc.at[1])
    klo_own.start()
    lat_away = pltpu.make_async_remote_copy(
        src_ref=lat_ref, dst_ref=latb.at[core], send_sem=misc.at[2], recv_sem=misc.at[3], device_id=partner, device_id_type=MESH
    )
    lat_away.start()
    klo_away = pltpu.make_async_remote_copy(
        src_ref=klo_ref, dst_ref=klob.at[core], send_sem=misc.at[4], recv_sem=misc.at[5], device_id=partner, device_id_type=MESH
    )
    klo_away.start()

    def group_of(step, half):
        dx, dy = gray(step % 4), gray(step // 4)
        return (((me.x + dx) % 4) * 2 + half) * 4 + (me.y + dy) % 4

    def columns(step, half, width):
        return pl.ds(pl.multiple_of(group_of(step, half) * width, width), width)

    def own_q(s):
        return pltpu.make_async_copy(q_hbm.at[:, columns(s, core, QW)], qbuf.at[s, core], loc_q.at[s])

    def own_go(s):
        return pltpu.make_async_copy(go_hbm.at[:, columns(s, core, VW)], gobuf.at[s, core], loc_go.at[s])

    def away_q(s):
        return pltpu.make_async_remote_copy(
            src_ref=q_hbm.at[:, columns(s, other, QW)],
            dst_ref=qbuf.at[s, core],
            send_sem=snd_q.at[s],
            recv_sem=rem_q.at[s],
            device_id=partner,
            device_id_type=MESH,
        )

    def away_go(s):
        return pltpu.make_async_remote_copy(
            src_ref=go_hbm.at[:, columns(s, other, VW)],
            dst_ref=gobuf.at[s, core],
            send_sem=snd_go.at[s],
            recv_sem=rem_go.at[s],
            device_id=partner,
            device_id_type=MESH,
        )

    def from_q(s):
        return pltpu.make_async_remote_copy(
            src_ref=q_hbm.at[:, columns(s, core, QW)],
            dst_ref=qbuf.at[s, other],
            send_sem=snd_q.at[s],
            recv_sem=rem_q.at[s],
            device_id=partner,
            device_id_type=MESH,
        )

    def from_go(s):
        return pltpu.make_async_remote_copy(
            src_ref=go_hbm.at[:, columns(s, core, VW)],
            dst_ref=gobuf.at[s, other],
            send_sem=snd_go.at[s],
            recv_sem=rem_go.at[s],
            device_id=partner,
            device_id_type=MESH,
        )

    def gather_copy(half, dx, dy, piece, axis, sign):
        first, count = rows_of(half, piece)
        there = (dx - sign, dy) if axis == "x" else (dx, dy - sign)
        there = (there[0] % 4, there[1] % 4)
        index = GATHER[(half, there[0], there[1], piece)]
        return pltpu.make_async_remote_copy(
            src_ref=wbuf.at[slot_of(dx, dy), pl.ds(first, count)],
            dst_ref=wbuf.at[slot_of(*there), pl.ds(first, count)],
            send_sem=ag_send.at[index],
            recv_sem=ag_recv.at[index],
            device_id=me.neighbour(axis, sign),
            device_id_type=MESH,
        )

    def gather_wait(half, dx, dy, piece):
        first, count = rows_of(half, piece)
        index = GATHER[(half, dx, dy, piece)]
        pltpu.make_async_remote_copy(
            src_ref=wbuf.at[slot_of(dx, dy), pl.ds(first, count)],
            dst_ref=wbuf.at[slot_of(dx, dy), pl.ds(first, count)],
            send_sem=ag_send.at[index],
            recv_sem=ag_recv.at[index],
            device_id=me.neighbour("x", 1),
            device_id_type=MESH,
        ).wait_recv()

    def gather_event(half, along, across):
        first_axis = main_axis(half)
        second_axis = "y" if first_axis == "x" else "x"
        dx, dy = at(first_axis, along, across)
        if along or across:
            last = across if across else along
            for piece in ("0", "1") if last == 2 else ("f",):
                gather_wait(half, dx, dy, piece)
        if across == 0:
            if along == 0:
                for sign in (1, -1):
                    gather_copy(half, dx, dy, "f", first_axis, sign).start()
            elif along == 3:
                gather_copy(half, dx, dy, "0", first_axis, 1).start()
            elif along == 1:
                gather_copy(half, dx, dy, "1", first_axis, -1).start()
            for sign in (1, -1):
                gather_copy(half, dx, dy, "f", second_axis, sign).start()
        elif across == 3:
            gather_copy(half, dx, dy, "0", second_axis, 1).start()
        elif across == 1:
            gather_copy(half, dx, dy, "1", second_axis, -1).start()

    def gather_sends():
        done = []
        for half in (0, 1):
            first_axis = main_axis(half)
            second_axis = "y" if first_axis == "x" else "x"
            for along in range(4):
                dx, dy = at(first_axis, along, 0)
                if along == 0:
                    done += [(half, dx, dy, "f", first_axis, 1), (half, dx, dy, "f", first_axis, -1)]
                elif along == 3:
                    done += [(half, dx, dy, "0", first_axis, 1)]
                elif along == 1:
                    done += [(half, dx, dy, "1", first_axis, -1)]
                done += [(half, dx, dy, "f", second_axis, 1), (half, dx, dy, "f", second_axis, -1)]
                dx, dy = at(first_axis, along, 3)
                done += [(half, dx, dy, "0", second_axis, 1)]
                dx, dy = at(first_axis, along, 1)
                done += [(half, dx, dy, "1", second_axis, -1)]
        return done

    events = {
        1: [(0, 1, 0), (0, 3, 0), (1, 1, 0), (1, 3, 0), (1, 0, 1)],
        2: [(1, 0, 3), (0, 0, 1), (0, 0, 3)],
        3: [(0, 2, 0), (1, 2, 0), (1, 0, 2)],
        4: [],
        5: [(0, 1, 1), (1, 1, 1)],
        6: [(0, 3, 1), (1, 1, 3)],
        7: [(0, 2, 1), (1, 1, 2)],
        8: [],
        9: [(0, 1, 3), (1, 3, 1)],
        10: [(0, 3, 3), (1, 3, 3)],
        11: [(0, 2, 3), (1, 3, 2)],
        12: [(0, 0, 2)],
        13: [(0, 1, 2), (1, 2, 1)],
        14: [(0, 3, 2), (1, 2, 3)],
        15: [(0, 2, 2), (1, 2, 2)],
    }

    @pl.when(is_source)
    def _():
        own = pltpu.make_async_copy(w_ref, wbuf.at[0], misc.at[6])
        own.start()
        own.wait()

    @pl.when(jnp.logical_not(is_source))
    def _():
        for half in (0, 1):
            z_copy(0, half).wait_recv()

    gather_event(0, 0, 0)
    gather_event(1, 0, 0)

    def start_tokens(s, carry):
        away_q(s).start()
        away_go(s).start()
        own_q(s).start()
        own_go(s).start()
        return carry

    lax.fori_loop(0, 16, start_tokens, 0)

    lat_own.wait()
    klo_own.wait()
    for trace in range(2):
        pass
    pltpu.make_async_remote_copy(
        src_ref=lat_ref, dst_ref=latb.at[other], send_sem=misc.at[2], recv_sem=misc.at[3], device_id=partner, device_id_type=MESH
    ).wait_recv()
    pltpu.make_async_remote_copy(
        src_ref=klo_ref, dst_ref=klob.at[other], send_sem=misc.at[4], recv_sem=misc.at[5], device_id=partner, device_id_type=MESH
    ).wait_recv()
    key = lax.broadcasted_iota(jnp.int32, (KEYS, OWN), 0)
    row = lax.broadcasted_iota(jnp.int32, (KEYS, OWN), 1)
    place = (key % STRETCH + STRETCH * (key // OWN)).astype(F32)
    latest = (STRETCH + row % STRETCH).astype(F32)
    same = ((key % OWN) // STRETCH) == (row // STRETCH)
    for trace in range(2):
        allowed = same & (place <= latest) & (place >= klob[trace, 0:1, :])
        bias[trace] = jnp.where(allowed, 0.0, -jnp.inf)
        lat_t[:, trace * KEYS : (trace + 1) * KEYS] = latb[trace, :, :D_LAT].T
    acc[...] = jnp.zeros_like(acc)

    def dot(a, b, ca=1, cb=0):
        return lax.dot_general(a, b, (((ca,), (cb,)), ((), ())), preferred_element_type=F32)

    def local_gq(s):
        return pltpu.make_async_copy(gqbuf.at[s, core], gq_hbm.at[:, columns(s, core, QW)], gq_loc.at[s])

    def away_gq(s):
        return pltpu.make_async_remote_copy(
            src_ref=gqbuf.at[s, other],
            dst_ref=gq_hbm.at[:, columns(s, core, QW)],
            send_sem=gq_snd.at[s],
            recv_sem=gq_rcv.at[s],
            device_id=partner,
            device_id_type=MESH,
        )

    def from_gq(s):
        return pltpu.make_async_remote_copy(
            src_ref=gqbuf.at[s, other],
            dst_ref=gq_hbm.at[:, columns(s, other, QW)],
            send_sem=gq_snd.at[s],
            recv_sem=gq_rcv.at[s],
            device_id=partner,
            device_id_type=MESH,
        )

    def step_body(s, carry):
        for at_step, todo in events.items():
            if todo:

                @pl.when(s == at_step)
                def _(todo=todo):
                    for event in todo:
                        gather_event(*event)

        own_q(s).wait()
        own_go(s).wait()
        from_q(s).wait_recv()
        from_go(s).wait_recv()
        for trace in range(2):
            kvbuf[trace * KEYS : (trace + 1) * KEYS, :] = dot(latb[trace, :, :D_LAT], wbuf[s]).astype(BF16)
        for trace in range(2):
            span = slice(trace * KEYS, (trace + 1) * KEYS)
            rope = latb[trace, :, D_LAT:]
            queries = qbuf[s, trace]
            grads = gobuf[s, trace]
            out = []
            grope = None
            for head in range(2):
                base = head * (D_NOPE + D_V)
                keys = jnp.concatenate([kvbuf[span, base : base + D_NOPE], rope], 1)
                values = kvbuf[span, base + D_NOPE : base + D_NOPE + D_V]
                query = queries[:, head * (D_NOPE + D_ROPE) : (head + 1) * (D_NOPE + D_ROPE)]
                grad = grads[:, head * D_V : (head + 1) * D_V]
                scores = dot(keys, query, 1, 1) * SCALE + bias[trace]
                highest = jnp.max(scores, 0, keepdims=True)
                expo = jnp.exp(scores - highest)
                probs = expo * (1.0 / jnp.sum(expo, 0, keepdims=True))
                dprob = dot(values, grad, 1, 1)
                delta = jnp.sum(probs * dprob, 0, keepdims=True)
                dscore = (probs * (dprob - delta) * SCALE).astype(BF16)
                gkey = dot(dscore, query)
                gkvbuf[span, base : base + D_NOPE] = gkey[:, :D_NOPE].astype(BF16)
                gkvbuf[span, base + D_NOPE : base + D_NOPE + D_V] = dot(probs.astype(BF16), grad).astype(BF16)
                grope = gkey[:, D_NOPE:] if grope is None else grope + gkey[:, D_NOPE:]
                out.append(dot(dscore, keys, 0, 0).astype(BF16))
            gqbuf[s, trace] = jnp.concatenate(out, 1)
            acc[trace, :, D_LAT:] += grope
        local_gq(s).start()
        away_gq(s).start()
        for trace in range(2):
            acc[trace, :, :D_LAT] += dot(gkvbuf[trace * KEYS : (trace + 1) * KEYS, :], wbuf[s], 1, 1)
        gbuf[s] = dot(lat_t[...], gkvbuf[...]).astype(BF16)
        return carry

    lax.fori_loop(0, 16, step_body, 0)

    acc_away = pltpu.make_async_remote_copy(
        src_ref=acc.at[other], dst_ref=accin, send_sem=misc.at[7], recv_sem=misc.at[8], device_id=partner, device_id_type=MESH
    )
    acc_away.start()

    def reduce_copy(half, phase, across, piece, axis, sign, dx, dy, rows, index_piece):
        first, count = rows
        index, row, _ = REDUCE[(half, phase, across, index_piece)]
        return pltpu.make_async_remote_copy(
            src_ref=gbuf.at[slot_of(dx, dy), pl.ds(first, count)],
            dst_ref=rbuf.at[pl.ds(row, count)],
            send_sem=rs_send.at[index],
            recv_sem=rs_recv.at[index],
            device_id=me.neighbour(axis, sign),
            device_id_type=MESH,
        )

    def reduce_plan(half, phase, across):
        first_axis = main_axis(half)
        second_axis = "y" if first_axis == "x" else "x"
        axis = second_axis if phase == 0 else first_axis

        def place_of(step):
            return at(first_axis, across, step) if phase == 0 else at(first_axis, step, 0)

        far, back, ahead = place_of(2), place_of(3), place_of(1)
        whole = rows_of(half, "f")
        return {
            "0": reduce_copy(half, phase, across, "0", axis, -1, *far, rows_of(half, "0"), "0"),
            "1": reduce_copy(half, phase, across, "1", axis, 1, *far, rows_of(half, "1"), "1"),
            "back": reduce_copy(half, phase, across, "f", axis, -1, *back, whole, "from1"),
            "ahead": reduce_copy(half, phase, across, "f", axis, 1, *ahead, whole, "from3"),
            "slots": (slot_of(*back), slot_of(*ahead), slot_of(*place_of(0))),
        }

    plans = {
        (half, phase, across): reduce_plan(half, phase, across)
        for half in (0, 1)
        for phase in (0, 1)
        for across in (range(4) if phase == 0 else (0,))
    }

    def add_rows(slot, first, count, sources):
        for start in range(0, count, 64):
            span = pl.ds(first + start, 64)
            total = gbuf[slot, span, :].astype(F32)
            for source in sources:
                total = total + rbuf[pl.ds(source + start, 64), :].astype(F32)
            gbuf[slot, span, :] = total.astype(BF16)

    def stage_far(half, phase, across):
        plan = plans[(half, phase, across)]
        plan["0"].start()
        plan["1"].start()

    def stage_near(half, phase, across):
        plan = plans[(half, phase, across)]
        back, ahead, _ = plan["slots"]
        for piece, slot, name in (("0", back, "back"), ("1", ahead, "ahead")):
            plan[piece].wait_recv()
            first, count = rows_of(half, piece)
            add_rows(slot, first, count, [REDUCE[(half, phase, across, piece)][1]])
            plan[name].start()

    def stage_own(half, phase, across):
        plan = plans[(half, phase, across)]
        plan["back"].wait_recv()
        plan["ahead"].wait_recv()
        first, count = rows_of(half, "f")
        own = plan["slots"][2]
        sources = [REDUCE[(half, phase, across, name)][1] for name in ("from1", "from3")]
        add_rows(own, first, count, sources)

    order = (2, 1, 3, 0)
    for across in order:
        for half in (0, 1):
            stage_far(half, 0, across)
    for across in order:
        for half in (0, 1):
            stage_near(half, 0, across)
    for across in order:
        for half in (0, 1):
            stage_own(half, 0, across)
        if across == 2:
            for half in (0, 1):
                stage_far(half, 1, 0)
    for half in (0, 1):
        stage_near(half, 1, 0)
    for half in (0, 1):
        stage_own(half, 1, 0)
    sum_ref[...] = gbuf[0]

    acc_away.wait_recv()
    for start in range(0, KEYS, 64):
        glat_ref[start : start + 64, :] = acc[core, start : start + 64, :] + accin[start : start + 64, :]

    def finish(s, carry):
        away_q(s).wait_send()
        away_go(s).wait_send()
        local_gq(s).wait()
        away_gq(s).wait_send()
        from_gq(s).wait_recv()
        return carry

    lax.fori_loop(0, 16, finish, 0)
    acc_away.wait_send()
    lat_away.wait_send()
    klo_away.wait_send()
    for args in gather_sends():
        gather_copy(*args).wait_send()
    for plan in plans.values():
        for name in ("0", "1", "back", "ahead"):
            plan[name].wait_send()

    @pl.when(sends_up)
    def _():
        for half in (0, 1):
            for zl in (0, 1):
                z_copy(zl, half).wait_send()

    @pl.when(sends_down)
    def _():
        for half in (0, 1):
            for zl in (3, 2):
                z_copy(zl, half).wait_send()


def main_call(queries, grad_out, lat, klo, weight):
    dma = pltpu.SemaphoreType.DMA
    any_spec = pl.BlockSpec(memory_space=pl.ANY)
    vmem = pl.BlockSpec(memory_space=pltpu.VMEM)
    return pl.pallas_call(
        main_kernel,
        out_shape=(
            jax.ShapeDtypeStruct(queries.shape, BF16),
            jax.ShapeDtypeStruct((KEYS, D_ALL), F32),
            jax.ShapeDtypeStruct((D_LAT, KVW), BF16),
        ),
        in_specs=[any_spec, any_spec, vmem, vmem, vmem],
        out_specs=(any_spec, vmem, vmem),
        scratch_shapes=[
            pltpu.VMEM((16, 2, OWN, QW), BF16),
            pltpu.VMEM((16, 2, OWN, VW), BF16),
            pltpu.VMEM((16, 2, OWN, QW), BF16),
            pltpu.VMEM((2, KEYS, D_ALL), BF16),
            pltpu.VMEM((D_LAT, 2 * KEYS), BF16),
            pltpu.VMEM((2, 8, OWN), F32),
            pltpu.VMEM((2, KEYS, OWN), F32),
            pltpu.VMEM((16, D_LAT, KVW), BF16),
            pltpu.VMEM((16, D_LAT, KVW), BF16),
            pltpu.VMEM((REDUCE_ROWS, KVW), BF16),
            pltpu.VMEM((2 * KEYS, KVW), BF16),
            pltpu.VMEM((2 * KEYS, KVW), BF16),
            pltpu.VMEM((2, KEYS, D_ALL), F32),
            pltpu.VMEM((KEYS, D_ALL), F32),
        ]
        + [dma((16,))] * 6
        + [dma((9,)), dma((6,))]
        + [dma((len(GATHER),))] * 2
        + [dma((len(REDUCE),))] * 2
        + [dma((16,))] * 3,
        compiler_params=pltpu.CompilerParams(collective_id=0, has_side_effects=True, vmem_limit_bytes=VMEM_LIMIT),
        cost_estimate=pl.CostEstimate(flops=16_000_000_000, bytes_accessed=12_000_000, transcendentals=2_000_000),
        name="attend",
    )(queries, grad_out, lat, klo, weight)


def z_kernel(part_ref, out_ref, parts, piece, pieces, send1, recv1, send2, recv2):
    me = Coords()
    mine = me.zh == me.core
    place = me.zh * 4 + me.zl

    barrier = pltpu.get_barrier_semaphore()
    everyone = [(zh, zl, core) for zh in (0, 1) for zl in range(4) for core in (0, 1)]
    def meets(zh, zl, core):
        same_core = core == me.core
        same_half = zh == me.zh
        itself = same_core & same_half & (zl == me.zl)
        return jnp.logical_and(jnp.logical_or(same_core, same_half), jnp.logical_not(itself))

    for zh, zl, core in everyone:

        @pl.when(meets(zh, zl, core))
        def _(zh=zh, zl=zl, core=core):
            pl.semaphore_signal(barrier, inc=1, device_id=me.device(zh=zh, zl=zl, core=core), device_id_type=MESH)

    pl.semaphore_wait(barrier, 11)

    def first(zl):
        return pltpu.make_async_remote_copy(
            src_ref=part_ref.at[pl.ds(zl * QUARTER, QUARTER)],
            dst_ref=parts.at[place],
            send_sem=send1.at[zl],
            recv_sem=recv1.at[place],
            device_id=me.device(zh=me.core, zl=zl),
            device_id_type=MESH,
        )

    for zl in range(4):

        @pl.when(jnp.logical_not(jnp.logical_and(mine, me.zl == zl)))
        def _(zl=zl):
            first(zl).start()

    def second(zl, core):
        return pltpu.make_async_remote_copy(
            src_ref=piece,
            dst_ref=pieces.at[me.zl],
            send_sem=send2.at[zl * 2 + core],
            recv_sem=recv2.at[me.zl],
            device_id=me.device(zl=zl, core=core),
            device_id_type=MESH,
        )

    def is_me(zl, core):
        return jnp.logical_and(me.zl == zl, me.core == core)

    @pl.when(mine)
    def _():
        for source in range(8):

            @pl.when(place != source)
            def _(source=source):
                pltpu.make_async_remote_copy(
                    src_ref=parts.at[source],
                    dst_ref=parts.at[source],
                    send_sem=send1.at[0],
                    recv_sem=recv1.at[source],
                    device_id=me.device(zh=me.core, zl=0),
                    device_id_type=MESH,
                ).wait_recv()

            @pl.when(place == source)
            def _(source=source):
                parts[source] = part_ref[pl.ds(pl.multiple_of(me.zl * QUARTER, QUARTER), QUARTER), :]

        for start in range(0, QUARTER, 64):
            total = parts[0, start : start + 64, :].astype(F32)
            for source in range(1, 8):
                total = total + parts[source, start : start + 64, :].astype(F32)
            piece[start : start + 64, :] = total.astype(BF16)
        for zl in range(4):
            for core in (0, 1):

                @pl.when(jnp.logical_not(is_me(zl, core)))
                def _(zl=zl, core=core):
                    second(zl, core).start()

    for zl in range(4):
        here = jnp.logical_and(mine, me.zl == zl)

        @pl.when(here)
        def _(zl=zl):
            out_ref[zl * QUARTER : (zl + 1) * QUARTER, :] = piece[...].astype(F32)

        @pl.when(jnp.logical_not(here))
        def _(zl=zl):
            pltpu.make_async_remote_copy(
                src_ref=piece,
                dst_ref=pieces.at[zl],
                send_sem=send2.at[0],
                recv_sem=recv2.at[zl],
                device_id=me.device(core=1 - me.core),
                device_id_type=MESH,
            ).wait_recv()
            out_ref[zl * QUARTER : (zl + 1) * QUARTER, :] = pieces[zl].astype(F32)

    for zl in range(4):

        @pl.when(jnp.logical_not(jnp.logical_and(mine, me.zl == zl)))
        def _(zl=zl):
            first(zl).wait_send()

        for core in (0, 1):

            @pl.when(jnp.logical_and(mine, jnp.logical_not(is_me(zl, core))))
            def _(zl=zl, core=core):
                second(zl, core).wait_send()


def z_call(part):
    dma = pltpu.SemaphoreType.DMA
    vmem = pl.BlockSpec(memory_space=pltpu.VMEM)
    return pl.pallas_call(
        z_kernel,
        out_shape=jax.ShapeDtypeStruct((D_LAT, KVW), F32),
        in_specs=[vmem],
        out_specs=vmem,
        scratch_shapes=[
            pltpu.VMEM((8, QUARTER, KVW), BF16),
            pltpu.VMEM((QUARTER, KVW), BF16),
            pltpu.VMEM((4, QUARTER, KVW), BF16),
            dma((4,)),
            dma((8,)),
            dma((8,)),
            dma((4,)),
        ],
        compiler_params=pltpu.CompilerParams(collective_id=1, has_side_effects=True, vmem_limit_bytes=VMEM_LIMIT),
        name="sum_z",
    )(part)


def spread(blocks):
    count = lax.axis_size("ctx")
    rows = STRETCH // count
    parts = blocks.reshape(2, count, rows * D_ALL).transpose(1, 0, 2)
    return lax.all_to_all(parts, "ctx", split_axis=0, concat_axis=0, tiled=True).reshape(2 * count, rows * D_ALL)


def collect(parts):
    count = lax.axis_size("ctx")
    rows = STRETCH // count
    parts = lax.all_to_all(parts.reshape(count, 2, rows * D_ALL), "ctx", split_axis=0, concat_axis=0, tiled=True)
    return parts.transpose(1, 0, 2).reshape(2 * STRETCH, D_ALL)


def per_device(queries, grad_out, latent, up_weight, doc_lengths, stretch_order):
    order = stretch_order[0]
    slots = jnp.arange(order.shape[0], dtype=jnp.int32)
    before = jnp.sum(jnp.where(order[None, :] == order[:, None] - 1, slots[None, :], 0), 1)
    after = jnp.sum(jnp.where(order[None, :] == order[:, None] + 1, slots[None, :], 0), 1)
    has_after = order < order.shape[0] - 1

    ends = jnp.cumsum(doc_lengths[0])
    starts = ends - doc_lengths[0]
    me = lax.axis_index("ctx")
    mine = lax.dynamic_slice_in_dim(order, 2 * me, 2)
    position = (mine[:, None] * STRETCH + jnp.arange(STRETCH, dtype=jnp.int32)[None, :]).reshape(OWN)
    start = jnp.max(jnp.where(starts[:, None] <= position[None, :], starts[:, None], 0), 0)
    klo = (start - jnp.repeat(mine, STRETCH) * STRETCH + STRETCH).astype(F32)
    klo = jnp.broadcast_to(klo[None, :], (8, OWN))

    own = latent[0]
    halo = collect(jnp.take(spread(own.reshape(2, STRETCH, D_ALL)), before, axis=0))
    lat = jnp.concatenate([halo, own], 0)
    gq, glat, part = main_call(queries[0], grad_out[0], lat, klo, up_weight)
    weight_grad = z_call(part)

    returned = jnp.take(spread(glat[:OWN].astype(BF16).reshape(2, STRETCH, D_ALL)), after, axis=0)
    returned = collect(jnp.where(has_after[:, None], returned, jnp.zeros_like(returned)))
    latent_grad = (glat[OWN:] + returned.astype(F32)).astype(BF16)
    return gq[None], latent_grad[None], weight_grad


def solution(mesh):
    in_specs = (
        P("dp", "ctx", None),
        P("dp", "ctx", None),
        P("dp", "ctx", None),
        P(None, "ctx"),
        P("dp", None),
        P("dp", None),
    )
    out_specs = (P("dp", "ctx", None), P("dp", "ctx", None), P(None, "ctx"))
    return jax.shard_map(per_device, mesh=mesh, in_specs=in_specs, out_specs=out_specs, check_vma=False)
```

```python
import jax
import jax.numpy as jnp
from jax import lax
from jax.experimental import pallas as pl
from jax.experimental.pallas import tpu as pltpu
from jax.sharding import PartitionSpec as P


BF16 = jnp.bfloat16
F32 = jnp.float32
MESH = pl.DeviceIdType.MESH

D_NOPE = 128
D_ROPE = 64
D_V = 128
D_LAT = 512
D_ALL = D_LAT + D_ROPE
STRETCH = 64
CUT = D_ALL // 8
OWN = 128
KEYS = 256
QW = 2 * (D_NOPE + D_ROPE)
VW = 2 * D_V
KVW = 2 * (D_NOPE + D_V)
SCALE = (D_NOPE + D_ROPE) ** -0.5
HALF = D_LAT // 2
QUARTER = D_LAT // 4
VMEM_LIMIT = 60 * 1024 * 1024


ORDER = [
    (1, 0), (0, 1), (1, 1), (1, 3), (3, 1), (2, 1), (1, 2), (2, 0),
    (0, 2), (2, 3), (3, 2), (2, 2), (3, 3), (3, 0), (0, 3), (0, 0),
]
OWN_SLOT = ORDER.index((0, 0))


def slot_of(dx, dy):
    return ORDER.index((dx % 4, dy % 4))


def pick(step, digits):
    low = sum(d * 4**i for i, d in enumerate(digits[:8]))
    high = sum(d * 4**i for i, d in enumerate(digits[8:]))
    return lax.shift_right_logical(jnp.where(step < 8, low, high), 2 * (step % 8)) % 4


def rows_of(half, piece):
    base = half * HALF
    if piece == "f":
        return base, HALF
    return base + int(piece) * QUARTER, QUARTER


def main_axis(half):
    return "x" if half == 0 else "y"


def at(axis, along, across):
    return (along, across) if axis == "x" else (across, along)


class Coords:
    def __init__(self):
        dp, ctx = lax.axis_index("dp"), lax.axis_index("ctx")
        self.dp, self.ctx = dp, ctx
        self.zl, self.core = dp // 2, dp % 2
        self.x, self.zh, self.y = ctx // 8, (ctx // 4) % 2, ctx % 4

    def device(self, x=None, y=None, zh=None, zl=None, core=None):
        x = self.x if x is None else x
        y = self.y if y is None else y
        zh = self.zh if zh is None else zh
        zl = self.zl if zl is None else zl
        core = self.core if core is None else core
        return (zl * 2 + core, (x * 2 + zh) * 4 + y)

    def neighbour(self, axis, sign):
        if axis == "x":
            return self.device(x=(self.x + 4 + sign) % 4)
        return self.device(y=(self.y + 4 + sign) % 4)


def gather_keys():
    keys = []
    for half in (0, 1):
        axis = main_axis(half)
        for across in range(4):
            for along in range(4):
                dx, dy = at(axis, along, across)
                if along == 0 and across == 0:
                    continue
                last = across if across else along
                for piece in ("0", "1") if last == 2 else ("f",):
                    keys.append((half, dx, dy, piece))
    return {key: i for i, key in enumerate(keys)}


GATHER = gather_keys()


def reduce_keys():
    keys, row = {}, 0
    for half in (0, 1):
        for across in range(4):
            for phase in (0, 1):
                if phase == 1 and across:
                    continue
                for piece, count in (("0", QUARTER), ("1", QUARTER), ("from1", HALF), ("from3", HALF)):
                    keys[(half, phase, across, piece)] = (len(keys), row, count)
                    row += count
    return keys, row


REDUCE, REDUCE_ROWS = reduce_keys()


def main_kernel(
    q_hbm,
    go_hbm,
    lat_ref,
    klo_ref,
    moves_ref,
    w_ref,
    gq_hbm,
    glat_ref,
    weight_ref,
    qbuf,
    gobuf,
    gqbuf,
    latb,
    lat_t,
    klob,
    bias,
    wbuf,
    gbuf,
    rbuf,
    kvbuf,
    gkvbuf,
    acc,
    accin,
    hb0,
    hb1,
    hb2,
    hb3,
    hb4,
    hb5,
    hb6,
    hb7,
    parts,
    pieces,
    loc_q,
    loc_go,
    rem_q,
    rem_go,
    snd_q,
    snd_go,
    misc,
    lat_sem,
    hsem,
    z_send,
    z_recv,
    wz,
    ag_send,
    ag_recv,
    rs_send,
    rs_recv,
    gq_loc,
    gq_snd,
    gq_rcv,
):
    me = Coords()
    core, other = me.core, 1 - me.core
    partner = me.device(core=other)
    is_source = me.zh == core
    sends_up = jnp.logical_and(is_source, me.zl == 3)
    sends_down = jnp.logical_and(is_source, me.zl == 0)
    place = me.zh * 4 + me.zl

    def ctx_device(away):
        return (me.dp, (me.ctx + away) % 32)

    barrier = pltpu.get_barrier_semaphore()

    def greet(away, carry):
        pl.semaphore_signal(barrier, inc=1, device_id=ctx_device(away), device_id_type=MESH)
        return carry

    lax.fori_loop(1, 32, greet, 0)
    for away in (1, 2, 3):
        for zh in (me.zh, 1 - me.zh):
            pl.semaphore_signal(
                barrier, inc=1, device_id=me.device(zh=zh, zl=(me.zl + away) % 4), device_id_type=MESH
            )
    pl.semaphore_signal(barrier, inc=1, device_id=partner, device_id_type=MESH)
    pl.semaphore_wait(barrier, 38)

    def z_copy(zl, half):
        return pltpu.make_async_remote_copy(
            src_ref=w_ref.at[pl.ds(half * HALF, HALF)],
            dst_ref=wbuf.at[OWN_SLOT, pl.ds(half * HALF, HALF)],
            send_sem=wz.at[half + 2 * (0 if zl in (0, 3) else 1)],
            recv_sem=wz.at[4 + half],
            device_id=me.device(zh=1 - me.zh, zl=zl),
            device_id_type=MESH,
        )

    @pl.when(sends_up)
    def _():
        for half in (0, 1):
            for zl in (0, 1):
                z_copy(zl, half).start()

    @pl.when(sends_down)
    def _():
        for half in (0, 1):
            for zl in (3, 2):
                z_copy(zl, half).start()

    def lat_copy(trace, first):
        index = 2 if first else 0
        return pltpu.make_async_remote_copy(
            src_ref=latb.at[trace, pl.ds(first, OWN)],
            dst_ref=latb.at[trace, pl.ds(first, OWN)],
            send_sem=lat_sem.at[index],
            recv_sem=lat_sem.at[index + 1],
            device_id=partner,
            device_id_type=MESH,
        )

    def klo_copy(trace):
        return pltpu.make_async_remote_copy(
            src_ref=klo_ref,
            dst_ref=klob.at[trace],
            send_sem=misc.at[4],
            recv_sem=misc.at[5],
            device_id=partner,
            device_id_type=MESH,
        )

    def group_of(step, half):
        dx, dy = pick(step, [d[0] for d in ORDER]), pick(step, [d[1] for d in ORDER])
        return (((me.x + dx) % 4) * 2 + half) * 4 + (me.y + dy) % 4

    def columns(step, half, width):
        return pl.ds(pl.multiple_of(group_of(step, half) * width, width), width)

    def own_q(s):
        return pltpu.make_async_copy(q_hbm.at[:, columns(s, core, QW)], qbuf.at[s, core], loc_q.at[s])

    def own_go(s):
        return pltpu.make_async_copy(go_hbm.at[:, columns(s, core, VW)], gobuf.at[s, core], loc_go.at[s])

    def away_q(s):
        return pltpu.make_async_remote_copy(
            src_ref=q_hbm.at[:, columns(s, other, QW)],
            dst_ref=qbuf.at[s, core],
            send_sem=snd_q.at[s],
            recv_sem=rem_q.at[s],
            device_id=partner,
            device_id_type=MESH,
        )

    def away_go(s):
        return pltpu.make_async_remote_copy(
            src_ref=go_hbm.at[:, columns(s, other, VW)],
            dst_ref=gobuf.at[s, core],
            send_sem=snd_go.at[s],
            recv_sem=rem_go.at[s],
            device_id=partner,
            device_id_type=MESH,
        )

    def from_q(s):
        return pltpu.make_async_remote_copy(
            src_ref=q_hbm.at[:, columns(s, core, QW)],
            dst_ref=qbuf.at[s, other],
            send_sem=snd_q.at[s],
            recv_sem=rem_q.at[s],
            device_id=partner,
            device_id_type=MESH,
        )

    def from_go(s):
        return pltpu.make_async_remote_copy(
            src_ref=go_hbm.at[:, columns(s, core, VW)],
            dst_ref=gobuf.at[s, other],
            send_sem=snd_go.at[s],
            recv_sem=rem_go.at[s],
            device_id=partner,
            device_id_type=MESH,
        )

    def gather_copy(half, dx, dy, piece, axis, sign):
        first, count = rows_of(half, piece)
        there = (dx - sign, dy) if axis == "x" else (dx, dy - sign)
        there = (there[0] % 4, there[1] % 4)
        index = GATHER[(half, there[0], there[1], piece)]
        return pltpu.make_async_remote_copy(
            src_ref=wbuf.at[slot_of(dx, dy), pl.ds(first, count)],
            dst_ref=wbuf.at[slot_of(*there), pl.ds(first, count)],
            send_sem=ag_send.at[index],
            recv_sem=ag_recv.at[index],
            device_id=me.neighbour(axis, sign),
            device_id_type=MESH,
        )

    def gather_wait(half, dx, dy, piece):
        first, count = rows_of(half, piece)
        index = GATHER[(half, dx, dy, piece)]
        pltpu.make_async_remote_copy(
            src_ref=wbuf.at[slot_of(dx, dy), pl.ds(first, count)],
            dst_ref=wbuf.at[slot_of(dx, dy), pl.ds(first, count)],
            send_sem=ag_send.at[index],
            recv_sem=ag_recv.at[index],
            device_id=me.neighbour("x", 1),
            device_id_type=MESH,
        ).wait_recv()

    def gather_event(half, along, across):
        first_axis = main_axis(half)
        second_axis = "y" if first_axis == "x" else "x"
        dx, dy = at(first_axis, along, across)
        if along or across:
            last = across if across else along
            for piece in ("0", "1") if last == 2 else ("f",):
                gather_wait(half, dx, dy, piece)
        if across == 0:
            if along == 0:
                for sign in (1, -1):
                    gather_copy(half, dx, dy, "f", first_axis, sign).start()
            elif along == 3:
                gather_copy(half, dx, dy, "0", first_axis, 1).start()
            elif along == 1:
                gather_copy(half, dx, dy, "1", first_axis, -1).start()
            for sign in (1, -1):
                gather_copy(half, dx, dy, "f", second_axis, sign).start()
        elif across == 3:
            gather_copy(half, dx, dy, "0", second_axis, 1).start()
        elif across == 1:
            gather_copy(half, dx, dy, "1", second_axis, -1).start()

    def gather_sends():
        done = []
        for half in (0, 1):
            first_axis = main_axis(half)
            second_axis = "y" if first_axis == "x" else "x"
            for along in range(4):
                dx, dy = at(first_axis, along, 0)
                if along == 0:
                    done += [(half, dx, dy, "f", first_axis, 1), (half, dx, dy, "f", first_axis, -1)]
                elif along == 3:
                    done += [(half, dx, dy, "0", first_axis, 1)]
                elif along == 1:
                    done += [(half, dx, dy, "1", first_axis, -1)]
                done += [(half, dx, dy, "f", second_axis, 1), (half, dx, dy, "f", second_axis, -1)]
                dx, dy = at(first_axis, along, 3)
                done += [(half, dx, dy, "0", second_axis, 1)]
                dx, dy = at(first_axis, along, 1)
                done += [(half, dx, dy, "1", second_axis, -1)]
        return done

    events = {
        0: [(0, 1, 0), (0, 3, 0), (1, 1, 0), (1, 3, 0), (1, 0, 1)],
        1: [(0, 0, 1), (1, 0, 3), (0, 0, 3)],
        2: [(0, 2, 0), (1, 2, 0), (0, 1, 1), (1, 1, 1)],
        3: [(0, 1, 3), (1, 3, 1)],
        4: [(0, 3, 1), (1, 1, 3)],
        5: [(0, 2, 1), (1, 1, 2), (0, 3, 3), (1, 3, 3)],
        6: [(0, 1, 2), (1, 2, 1)],
        7: [(1, 0, 2), (0, 2, 3), (1, 2, 3)],
        8: [(0, 0, 2)],
        9: [(1, 3, 2)],
        10: [(0, 3, 2)],
        11: [(0, 2, 2), (1, 2, 2)],
    }

    def round_copy(source, dest, sems, away):
        to = (me.ctx + away) % 32
        return pltpu.make_async_remote_copy(
            src_ref=source.at[pl.ds(2 * to, 2)],
            dst_ref=dest.at[pl.ds(2 * me.ctx, 2)],
            send_sem=sems[0].at[away],
            recv_sem=sems[1].at[away],
            device_id=ctx_device(away),
            device_id_type=MESH,
        )

    def round_start(source, dest, sems):
        def go(away, carry):
            round_copy(source, dest, sems, away).start()
            return carry

        lax.fori_loop(1, 32, go, 0)
        for t in range(2):
            dest[2 * me.ctx + t] = source[2 * me.ctx + t]

    def round_wait(source, dest, sems):
        def go(away, carry):
            frm = (me.ctx + 32 - away) % 32
            pltpu.make_async_remote_copy(
                src_ref=source.at[pl.ds(2 * frm, 2)],
                dst_ref=dest.at[pl.ds(2 * frm, 2)],
                send_sem=sems[0].at[away],
                recv_sem=sems[1].at[away],
                device_id=ctx_device(away),
                device_id_type=MESH,
            ).wait_recv()
            return carry

        lax.fori_loop(1, 32, go, 0)

    def round_end(source, dest, sems):
        def go(away, carry):
            round_copy(source, dest, sems, away).wait_send()
            return carry

        lax.fori_loop(1, 32, go, 0)

    def cut(read, dest):
        for i in range(4):
            for t in range(2):
                rows = read(t * STRETCH + 16 * i, 16)
                for j in range(8):
                    dest[2 * (8 * i + j) + t] = rows[:, CUT * j : CUT * (j + 1)]

    def join(source, t, i):
        return jnp.concatenate([source[2 * (8 * i + j) + t] for j in range(8)], 1)

    hbuf = (hb0, hb1, hb2, hb3, hb4, hb5, hb6, hb7)
    rounds = [(hsem.at[2 * i], hsem.at[2 * i + 1]) for i in range(4)]
    cut(lambda first, count: lat_ref[first : first + count, :], hb0)
    round_start(hb0, hb1, rounds[0])

    latb[core, OWN:, :] = lat_ref[...]
    lat_copy(core, OWN).start()
    klob[core] = klo_ref[...]
    klo_copy(core).start()

    @pl.when(is_source)
    def _():
        wbuf[OWN_SLOT] = w_ref[...]

    @pl.when(jnp.logical_not(is_source))
    def _():
        for half in (0, 1):
            z_copy(0, half).wait_recv()

    gather_event(0, 0, 0)
    gather_event(1, 0, 0)

    def start_tokens(s, carry):
        away_q(s).start()
        away_go(s).start()
        own_q(s).start()
        own_go(s).start()
        return carry

    lax.fori_loop(0, 16, start_tokens, 0)

    round_wait(hb0, hb1, rounds[0])
    for s in range(64):
        hb2[s] = hb1[moves_ref[0, s]]
    round_start(hb2, hb3, rounds[1])

    klo_copy(other).wait_recv()
    key = lax.broadcasted_iota(jnp.int32, (KEYS, OWN), 0)
    row = lax.broadcasted_iota(jnp.int32, (KEYS, OWN), 1)
    spot = (key % STRETCH + STRETCH * (key // OWN)).astype(F32)
    latest = (STRETCH + row % STRETCH).astype(F32)
    same = ((key % OWN) // STRETCH) == (row // STRETCH)
    for trace in range(2):
        allowed = same & (spot <= latest) & (spot >= klob[trace, 0:1, :])
        bias[trace] = jnp.where(allowed, 0.0, -jnp.inf)
    acc[...] = jnp.zeros_like(acc)

    round_wait(hb2, hb3, rounds[1])
    for t in range(2):
        for i in range(4):
            first = t * STRETCH + 16 * i
            latb[core, first : first + 16, :] = join(hb3, t, i)
    lat_copy(core, 0).start()
    lat_copy(other, OWN).wait_recv()
    lat_copy(other, 0).wait_recv()
    for trace in range(2):
        lat_t[:, trace * KEYS : (trace + 1) * KEYS] = latb[trace, :, :D_LAT].T

    def dot(a, b, ca=1, cb=0):
        return lax.dot_general(a, b, (((ca,), (cb,)), ((), ())), preferred_element_type=F32)

    def local_gq(s):
        return pltpu.make_async_copy(gqbuf.at[s, core], gq_hbm.at[:, columns(s, core, QW)], gq_loc.at[s])

    def away_gq(s):
        return pltpu.make_async_remote_copy(
            src_ref=gqbuf.at[s, other],
            dst_ref=gq_hbm.at[:, columns(s, core, QW)],
            send_sem=gq_snd.at[s],
            recv_sem=gq_rcv.at[s],
            device_id=partner,
            device_id_type=MESH,
        )

    def from_gq(s):
        return pltpu.make_async_remote_copy(
            src_ref=gqbuf.at[s, other],
            dst_ref=gq_hbm.at[:, columns(s, other, QW)],
            send_sem=gq_snd.at[s],
            recv_sem=gq_rcv.at[s],
            device_id=partner,
            device_id_type=MESH,
        )

    def reduce_copy(half, phase, across, piece, axis, sign, dx, dy, rows, index_piece):
        first, count = rows
        index, row, _ = REDUCE[(half, phase, across, index_piece)]
        return pltpu.make_async_remote_copy(
            src_ref=gbuf.at[slot_of(dx, dy), pl.ds(first, count)],
            dst_ref=rbuf.at[pl.ds(row, count)],
            send_sem=rs_send.at[index],
            recv_sem=rs_recv.at[index],
            device_id=me.neighbour(axis, sign),
            device_id_type=MESH,
        )

    def reduce_plan(half, phase, across):
        first_axis = main_axis(half)
        second_axis = "y" if first_axis == "x" else "x"
        axis = second_axis if phase == 0 else first_axis

        def place_of(step):
            return at(first_axis, across, step) if phase == 0 else at(first_axis, step, 0)

        far, back, ahead = place_of(2), place_of(3), place_of(1)
        whole = rows_of(half, "f")
        return {
            "0": reduce_copy(half, phase, across, "0", axis, -1, *far, rows_of(half, "0"), "0"),
            "1": reduce_copy(half, phase, across, "1", axis, 1, *far, rows_of(half, "1"), "1"),
            "back": reduce_copy(half, phase, across, "f", axis, -1, *back, whole, "from1"),
            "ahead": reduce_copy(half, phase, across, "f", axis, 1, *ahead, whole, "from3"),
            "slots": (slot_of(*back), slot_of(*ahead), slot_of(*place_of(0))),
        }

    plans = {
        (half, phase, across): reduce_plan(half, phase, across)
        for half in (0, 1)
        for phase in (0, 1)
        for across in (range(4) if phase == 0 else (0,))
    }

    def add_rows(slot, first, count, sources):
        def go(i, carry):
            start = pl.multiple_of(i * 32, 32)
            span = pl.ds(first + start, 32)
            total = gbuf[slot, span, :].astype(F32)
            for source in sources:
                total = total + rbuf[pl.ds(source + start, 32), :].astype(F32)
            gbuf[slot, span, :] = total.astype(BF16)
            return carry

        lax.fori_loop(0, count // 32, go, 0)

    def stage_far(half, phase, across):
        plan = plans[(half, phase, across)]
        plan["0"].start()
        plan["1"].start()

    def stage_near(half, phase, across):
        plan = plans[(half, phase, across)]
        back, ahead, _ = plan["slots"]
        for piece, slot, name in (("0", back, "back"), ("1", ahead, "ahead")):
            plan[piece].wait_recv()
            first, count = rows_of(half, piece)
            add_rows(slot, first, count, [REDUCE[(half, phase, across, piece)][1]])
            plan[name].start()

    def stage_own(half, phase, across):
        plan = plans[(half, phase, across)]
        plan["back"].wait_recv()
        plan["ahead"].wait_recv()
        first, count = rows_of(half, "f")
        own = plan["slots"][2]
        sources = [REDUCE[(half, phase, across, name)][1] for name in ("from1", "from3")]
        add_rows(own, first, count, sources)

    sums = {
        5: [(stage_far, 1, 1)],
        6: [(stage_far, 0, 1)],
        7: [(stage_far, 1, 0), (stage_near, 1, 1)],
        8: [(stage_far, 0, 0), (stage_near, 0, 1)],
        9: [(stage_far, 1, 3), (stage_own, 1, 1)],
        10: [(stage_far, 0, 3), (stage_own, 0, 1)],
        11: [(stage_far, 0, 2), (stage_far, 1, 2)],
        12: [(stage_near, 1, 3), (stage_near, 0, 3)],
        13: [(stage_near, 0, 2), (stage_near, 1, 2), (stage_near, 1, 0)],
        14: [(stage_near, 0, 0), (stage_own, 0, 3), (stage_own, 1, 3)],
    }

    def step_body(s, carry):
        for at_step, todo in events.items():
            if todo:

                @pl.when(s == at_step)
                def _(todo=todo):
                    for event in todo:
                        gather_event(*event)

        own_q(s).wait()
        own_go(s).wait()
        from_q(s).wait_recv()
        from_go(s).wait_recv()
        for trace in range(2):
            kvbuf[trace * KEYS : (trace + 1) * KEYS, :] = dot(latb[trace, :, :D_LAT], wbuf[s]).astype(BF16)
        for trace in range(2):
            span = slice(trace * KEYS, (trace + 1) * KEYS)
            rope = latb[trace, :, D_LAT:]
            queries = qbuf[s, trace]
            grads = gobuf[s, trace]
            out = []
            grope = None
            for head in range(2):
                base = head * (D_NOPE + D_V)
                keys = jnp.concatenate([kvbuf[span, base : base + D_NOPE], rope], 1)
                values = kvbuf[span, base + D_NOPE : base + D_NOPE + D_V]
                query = queries[:, head * (D_NOPE + D_ROPE) : (head + 1) * (D_NOPE + D_ROPE)]
                grad = grads[:, head * D_V : (head + 1) * D_V]
                scores = dot(keys, query, 1, 1) * SCALE + bias[trace]
                highest = jnp.max(scores, 0, keepdims=True)
                expo = jnp.exp(scores - highest)
                probs = expo * (1.0 / jnp.sum(expo, 0, keepdims=True))
                dprob = dot(values, grad, 1, 1)
                delta = jnp.sum(probs * dprob, 0, keepdims=True)
                dscore = (probs * (dprob - delta) * SCALE).astype(BF16)
                gkey = dot(dscore, query)
                gkvbuf[span, base : base + D_NOPE] = gkey[:, :D_NOPE].astype(BF16)
                gkvbuf[span, base + D_NOPE : base + D_NOPE + D_V] = dot(probs.astype(BF16), grad).astype(BF16)
                grope = gkey[:, D_NOPE:] if grope is None else grope + gkey[:, D_NOPE:]
                out.append(dot(dscore, keys, 0, 0).astype(BF16))
            gqbuf[s, trace] = jnp.concatenate(out, 1)
            acc[trace, :, D_LAT:] += grope
        local_gq(s).start()
        away_gq(s).start()
        for trace in range(2):
            acc[trace, :, :D_LAT] += dot(gkvbuf[trace * KEYS : (trace + 1) * KEYS, :], wbuf[s], 1, 1)
        gbuf[s] = dot(lat_t[...], gkvbuf[...]).astype(BF16)
        for at_step, todo in sums.items():

            @pl.when(s == at_step)
            def _(todo=todo):
                for stage, half, across in todo:
                    stage(half, 0, across)

        return carry

    lax.fori_loop(0, 16, step_body, 0)

    acc_away = pltpu.make_async_remote_copy(
        src_ref=acc.at[other], dst_ref=accin, send_sem=misc.at[0], recv_sem=misc.at[1], device_id=partner, device_id_type=MESH
    )
    acc_away.start()

    for half in (0, 1):
        stage_own(half, 0, 2)
        stage_far(half, 1, 0)
    for half in (0, 1):
        stage_own(half, 0, 0)

    acc_away.wait_recv()
    cut(
        lambda first, count: (acc[core, first : first + count, :] + accin[first : first + count, :]).astype(BF16),
        hb4,
    )
    round_start(hb4, hb5, rounds[2])
    for half in (0, 1):
        stage_near(half, 1, 0)

    def z_first(zl):
        return pltpu.make_async_remote_copy(
            src_ref=gbuf.at[OWN_SLOT, pl.ds(zl * QUARTER, QUARTER)],
            dst_ref=parts.at[place],
            send_sem=z_send.at[zl],
            recv_sem=z_recv.at[place],
            device_id=me.device(zh=core, zl=zl),
            device_id_type=MESH,
        )

    def not_mine(zl):
        return jnp.logical_not(jnp.logical_and(is_source, me.zl == zl))

    for half in (0, 1):
        stage_own(half, 1, 0)
        for zl in (2 * half, 2 * half + 1):

            @pl.when(not_mine(zl))
            def _(zl=zl):
                z_first(zl).start()

    round_wait(hb4, hb5, rounds[2])
    for s in range(64):
        moved = hb5[moves_ref[1, s]]
        hb6[s] = jnp.where(moves_ref[2, s] > 0, moved, jnp.zeros_like(moved))
    round_start(hb6, hb7, rounds[3])

    def z_second(zl):
        return pltpu.make_async_remote_copy(
            src_ref=pieces.at[me.zl],
            dst_ref=pieces.at[me.zl],
            send_sem=z_send.at[4 + zl],
            recv_sem=z_recv.at[8 + me.zl],
            device_id=me.device(zl=zl),
            device_id_type=MESH,
        )

    def z_third(zl):
        return pltpu.make_async_remote_copy(
            src_ref=pieces.at[zl],
            dst_ref=pieces.at[zl],
            send_sem=z_send.at[8 + zl],
            recv_sem=z_recv.at[12 + zl],
            device_id=partner,
            device_id_type=MESH,
        )

    @pl.when(is_source)
    def _():
        for source in range(8):

            @pl.when(place != source)
            def _(source=source):
                pltpu.make_async_remote_copy(
                    src_ref=parts.at[source],
                    dst_ref=parts.at[source],
                    send_sem=z_send.at[0],
                    recv_sem=z_recv.at[source],
                    device_id=partner,
                    device_id_type=MESH,
                ).wait_recv()

        parts[place] = gbuf[OWN_SLOT, pl.ds(pl.multiple_of(me.zl * QUARTER, QUARTER), QUARTER), :]

        def total_rows(i, carry):
            span = pl.ds(pl.multiple_of(i * 16, 16), 16)
            total = parts[0, span, :].astype(F32)
            for source in range(1, 8):
                total = total + parts[source, span, :].astype(F32)
            pieces[me.zl, span, :] = total.astype(BF16)
            return carry

        lax.fori_loop(0, QUARTER // 16, total_rows, 0)
        for zl in range(4):

            @pl.when(me.zl != zl)
            def _(zl=zl):
                z_second(zl).start()

        for away in range(4):
            zl = (me.zl + away) % 4
            if away:
                pltpu.make_async_remote_copy(
                    src_ref=pieces.at[zl],
                    dst_ref=pieces.at[zl],
                    send_sem=z_send.at[4],
                    recv_sem=z_recv.at[8 + zl],
                    device_id=partner,
                    device_id_type=MESH,
                ).wait_recv()
            z_third(zl).start()

    round_wait(hb6, hb7, rounds[3])
    for t in range(2):
        for i in range(4):
            first = t * STRETCH + 16 * i
            span = slice(OWN + first, OWN + first + 16)
            total = acc[core, span, :] + accin[span, :] + join(hb7, t, i).astype(F32)
            glat_ref[first : first + 16, :] = total.astype(BF16)

    @pl.when(jnp.logical_not(is_source))
    def _():
        for zl in range(4):
            z_third(zl).wait_recv()

    for zl in range(4):
        weight_ref[zl * QUARTER : (zl + 1) * QUARTER, :] = pieces[zl].astype(F32)

    def finish(s, carry):
        away_q(s).wait_send()
        away_go(s).wait_send()
        local_gq(s).wait()
        away_gq(s).wait_send()
        from_gq(s).wait_recv()
        return carry

    lax.fori_loop(0, 16, finish, 0)
    acc_away.wait_send()
    lat_copy(core, OWN).wait_send()
    lat_copy(core, 0).wait_send()
    klo_copy(core).wait_send()
    for i in range(4):
        round_end(hbuf[2 * i], hbuf[2 * i + 1], rounds[i])
    for zl in range(4):

        @pl.when(not_mine(zl))
        def _(zl=zl):
            z_first(zl).wait_send()

        @pl.when(jnp.logical_and(is_source, me.zl != zl))
        def _(zl=zl):
            z_second(zl).wait_send()

        @pl.when(is_source)
        def _(zl=zl):
            z_third(zl).wait_send()

    for args in gather_sends():
        gather_copy(*args).wait_send()
    for plan in plans.values():
        for name in ("0", "1", "back", "ahead"):
            plan[name].wait_send()

    @pl.when(sends_up)
    def _():
        for half in (0, 1):
            for zl in (0, 1):
                z_copy(zl, half).wait_send()

    @pl.when(sends_down)
    def _():
        for half in (0, 1):
            for zl in (3, 2):
                z_copy(zl, half).wait_send()


def main_call(queries, grad_out, latent, klo, moves, weight):
    dma = pltpu.SemaphoreType.DMA
    any_spec = pl.BlockSpec(memory_space=pl.ANY)
    vmem = pl.BlockSpec(memory_space=pltpu.VMEM)
    smem = pl.BlockSpec(memory_space=pltpu.SMEM)
    return pl.pallas_call(
        main_kernel,
        out_shape=(
            jax.ShapeDtypeStruct(queries.shape, BF16),
            jax.ShapeDtypeStruct(latent.shape, BF16),
            jax.ShapeDtypeStruct(weight.shape, F32),
        ),
        in_specs=[any_spec, any_spec, vmem, vmem, smem, vmem],
        out_specs=(any_spec, vmem, vmem),
        scratch_shapes=[
            pltpu.VMEM((16, 2, OWN, QW), BF16),
            pltpu.VMEM((16, 2, OWN, VW), BF16),
            pltpu.VMEM((16, 2, OWN, QW), BF16),
            pltpu.VMEM((2, KEYS, D_ALL), BF16),
            pltpu.VMEM((D_LAT, 2 * KEYS), BF16),
            pltpu.VMEM((2, 8, OWN), F32),
            pltpu.VMEM((2, KEYS, OWN), F32),
            pltpu.VMEM((16, D_LAT, KVW), BF16),
            pltpu.VMEM((16, D_LAT, KVW), BF16),
            pltpu.VMEM((REDUCE_ROWS, KVW), BF16),
            pltpu.VMEM((2 * KEYS, KVW), BF16),
            pltpu.VMEM((2 * KEYS, KVW), BF16),
            pltpu.VMEM((2, KEYS, D_ALL), F32),
            pltpu.VMEM((KEYS, D_ALL), F32),
            *[pltpu.VMEM((64, 16, CUT), BF16)] * 8,
            pltpu.VMEM((8, QUARTER, KVW), BF16),
            pltpu.VMEM((4, QUARTER, KVW), BF16),
        ]
        + [dma((16,))] * 6
        + [dma((6,)), dma((4,)), dma((8, 32)), dma((12,)), dma((16,)), dma((6,))]
        + [dma((len(GATHER),))] * 2
        + [dma((len(REDUCE),))] * 2
        + [dma((16,))] * 3,
        compiler_params=pltpu.CompilerParams(collective_id=0, has_side_effects=True, vmem_limit_bytes=VMEM_LIMIT),
        cost_estimate=pl.CostEstimate(flops=16_000_000_000, bytes_accessed=12_000_000, transcendentals=2_000_000),
        name="attend",
    )(queries, grad_out, latent, klo, moves, weight)


def per_device(queries, grad_out, latent, up_weight, doc_lengths, stretch_order):
    order = stretch_order[0]
    slots = jnp.arange(order.shape[0], dtype=jnp.int32)
    before = jnp.sum(jnp.where(order[None, :] == order[:, None] - 1, slots[None, :], 0), 1)
    after = jnp.sum(jnp.where(order[None, :] == order[:, None] + 1, slots[None, :], 0), 1)
    has_after = order < order.shape[0] - 1

    ends = jnp.cumsum(doc_lengths[0])
    starts = ends - doc_lengths[0]
    me = lax.axis_index("ctx")
    mine = lax.dynamic_slice_in_dim(order, 2 * me, 2)
    position = (mine[:, None] * STRETCH + jnp.arange(STRETCH, dtype=jnp.int32)[None, :]).reshape(OWN)
    start = jnp.max(jnp.where(starts[:, None] <= position[None, :], starts[:, None], 0), 0)
    klo = (start - jnp.repeat(mine, STRETCH) * STRETCH + STRETCH).astype(F32)
    klo = jnp.broadcast_to(klo[None, :], (8, OWN))

    moves = jnp.stack([before, after, has_after.astype(jnp.int32)])
    gq, latent_grad, weight_grad = main_call(queries[0], grad_out[0], latent[0], klo, moves, up_weight)
    return gq[None], latent_grad[None], weight_grad


def solution(mesh):
    in_specs = (
        P("dp", "ctx", None),
        P("dp", "ctx", None),
        P("dp", "ctx", None),
        P(None, "ctx"),
        P("dp", None),
        P("dp", None),
    )
    out_specs = (P("dp", "ctx", None), P("dp", "ctx", None), P(None, "ctx"))
    return jax.shard_map(per_device, mesh=mesh, in_specs=in_specs, out_specs=out_specs, check_vma=False)
```

```python
import jax
import jax.numpy as jnp
from jax import lax
from jax.experimental import pallas as pl
from jax.experimental.pallas import tpu as pltpu
from jax.sharding import PartitionSpec as P


BF16 = jnp.bfloat16
F32 = jnp.float32
MESH = pl.DeviceIdType.MESH

D_NOPE = 128
D_ROPE = 64
D_V = 128
D_LAT = 512
D_ALL = D_LAT + D_ROPE
STRETCH = 64
CUT = D_ALL // 8
OWN = 128
KEYS = 256
QW = 2 * (D_NOPE + D_ROPE)
VW = 2 * D_V
KVW = 2 * (D_NOPE + D_V)
SCALE = (D_NOPE + D_ROPE) ** -0.5
HALF = D_LAT // 2
QUARTER = D_LAT // 4
VMEM_LIMIT = 60 * 1024 * 1024


ORDER = [
    (1, 0), (0, 1), (1, 1), (1, 3), (3, 1), (2, 1), (1, 2), (2, 3),
    (3, 2), (2, 2), (2, 0), (0, 2), (3, 3), (3, 0), (0, 3), (0, 0),
]
OWN_SLOT = ORDER.index((0, 0))


def slot_of(dx, dy):
    return ORDER.index((dx % 4, dy % 4))


def pick(step, digits):
    low = sum(d * 4**i for i, d in enumerate(digits[:8]))
    high = sum(d * 4**i for i, d in enumerate(digits[8:]))
    return lax.shift_right_logical(jnp.where(step < 8, low, high), 2 * (step % 8)) % 4


def rows_of(half, piece):
    base = half * HALF
    if piece == "f":
        return base, HALF
    return base + int(piece) * QUARTER, QUARTER


def main_axis(half):
    return "x" if half == 0 else "y"


def at(axis, along, across):
    return (along, across) if axis == "x" else (across, along)


class Coords:
    def __init__(self):
        dp, ctx = lax.axis_index("dp"), lax.axis_index("ctx")
        self.dp, self.ctx = dp, ctx
        self.zl, self.core = dp // 2, dp % 2
        self.x, self.zh, self.y = ctx // 8, (ctx // 4) % 2, ctx % 4

    def device(self, x=None, y=None, zh=None, zl=None, core=None):
        x = self.x if x is None else x
        y = self.y if y is None else y
        zh = self.zh if zh is None else zh
        zl = self.zl if zl is None else zl
        core = self.core if core is None else core
        return (zl * 2 + core, (x * 2 + zh) * 4 + y)

    def neighbour(self, axis, sign):
        if axis == "x":
            return self.device(x=(self.x + 4 + sign) % 4)
        return self.device(y=(self.y + 4 + sign) % 4)


def gather_keys():
    keys = []
    for half in (0, 1):
        axis = main_axis(half)
        for across in range(4):
            for along in range(4):
                dx, dy = at(axis, along, across)
                if along == 0 and across == 0:
                    continue
                last = across if across else along
                for piece in ("0", "1") if last == 2 else ("f",):
                    keys.append((half, dx, dy, piece))
    return {key: i for i, key in enumerate(keys)}


GATHER = gather_keys()


def reduce_keys():
    keys, row = {}, 0
    for half in (0, 1):
        for across in range(4):
            for phase in (0, 1):
                if phase == 1 and across:
                    continue
                for piece, count in (("0", QUARTER), ("1", QUARTER), ("from1", HALF), ("from3", HALF)):
                    keys[(half, phase, across, piece)] = (len(keys), row, count)
                    row += count
    return keys, row


REDUCE, REDUCE_ROWS = reduce_keys()


def main_kernel(
    q_hbm,
    go_hbm,
    lat_ref,
    lens_ref,
    order_ref,
    moves_ref,
    w_ref,
    gq_hbm,
    glat_ref,
    weight_ref,
    qbuf,
    gobuf,
    gqbuf,
    latb,
    lat_t,
    klob,
    bias,
    wbuf,
    gbuf,
    rbuf,
    kvbuf,
    gkvbuf,
    acc,
    accin,
    hb0,
    hb1,
    hb2,
    hb3,
    hb4,
    hb5,
    hb6,
    hb7,
    parts,
    pieces,
    loc_q,
    loc_go,
    rem_q,
    rem_go,
    snd_q,
    snd_go,
    misc,
    lat_sem,
    hsem,
    z_send,
    z_recv,
    wz,
    ag_send,
    ag_recv,
    rs_send,
    rs_recv,
    gq_loc,
    gq_snd,
    gq_rcv,
):
    me = Coords()
    core, other = me.core, 1 - me.core
    partner = me.device(core=other)
    is_source = me.zh == core
    at_end = jnp.logical_or(me.zl == 0, me.zl == 3)
    z_sends = jnp.logical_and(is_source, at_end)
    z_forwards = jnp.logical_and(jnp.logical_not(is_source), at_end)
    place = me.zh * 4 + me.zl

    def ctx_device(away):
        return (me.dp, (me.ctx + away) % 32)

    barrier = pltpu.get_barrier_semaphore()

    def greet(away, carry):
        pl.semaphore_signal(barrier, inc=1, device_id=ctx_device(away), device_id_type=MESH)
        return carry

    lax.fori_loop(1, 32, greet, 0)
    for away in (1, 2, 3):
        for zh in (me.zh, 1 - me.zh):
            pl.semaphore_signal(
                barrier, inc=1, device_id=me.device(zh=zh, zl=(me.zl + away) % 4), device_id_type=MESH
            )
    pl.semaphore_signal(barrier, inc=1, device_id=partner, device_id_type=MESH)
    pl.semaphore_wait(barrier, 38)

    def z_copy(source, zh, zl, half):
        return pltpu.make_async_remote_copy(
            src_ref=source.at[pl.ds(half * HALF, HALF)],
            dst_ref=wbuf.at[OWN_SLOT, pl.ds(half * HALF, HALF)],
            send_sem=wz.at[half],
            recv_sem=wz.at[2 + half],
            device_id=me.device(zh=zh, zl=zl),
            device_id_type=MESH,
        )

    def z_send_copy(half):
        return z_copy(w_ref, 1 - me.zh, jnp.where(me.zl == 3, 0, 3), half)

    def z_forward(half):
        return z_copy(wbuf.at[OWN_SLOT], me.zh, jnp.where(me.zl == 0, 1, 2), half)

    @pl.when(z_sends)
    def _():
        for half in (0, 1):
            z_send_copy(half).start()

    def lat_copy(trace, first):
        index = 2 if first else 0
        return pltpu.make_async_remote_copy(
            src_ref=latb.at[trace, pl.ds(first, OWN)],
            dst_ref=latb.at[trace, pl.ds(first, OWN)],
            send_sem=lat_sem.at[index],
            recv_sem=lat_sem.at[index + 1],
            device_id=partner,
            device_id_type=MESH,
        )

    def klo_copy(trace):
        return pltpu.make_async_remote_copy(
            src_ref=klob.at[trace],
            dst_ref=klob.at[trace],
            send_sem=misc.at[2],
            recv_sem=misc.at[3],
            device_id=partner,
            device_id_type=MESH,
        )

    def group_of(step, half):
        dx, dy = pick(step, [d[0] for d in ORDER]), pick(step, [d[1] for d in ORDER])
        return (((me.x + dx) % 4) * 2 + half) * 4 + (me.y + dy) % 4

    def columns(step, half, width):
        return pl.ds(pl.multiple_of(group_of(step, half) * width, width), width)

    def own_q(s):
        return pltpu.make_async_copy(q_hbm.at[:, columns(s, core, QW)], qbuf.at[s, core], loc_q.at[s])

    def own_go(s):
        return pltpu.make_async_copy(go_hbm.at[:, columns(s, core, VW)], gobuf.at[s, core], loc_go.at[s])

    def away_q(s):
        return pltpu.make_async_remote_copy(
            src_ref=q_hbm.at[:, columns(s, other, QW)],
            dst_ref=qbuf.at[s, core],
            send_sem=snd_q.at[s],
            recv_sem=rem_q.at[s],
            device_id=partner,
            device_id_type=MESH,
        )

    def away_go(s):
        return pltpu.make_async_remote_copy(
            src_ref=go_hbm.at[:, columns(s, other, VW)],
            dst_ref=gobuf.at[s, core],
            send_sem=snd_go.at[s],
            recv_sem=rem_go.at[s],
            device_id=partner,
            device_id_type=MESH,
        )

    def from_q(s):
        return pltpu.make_async_remote_copy(
            src_ref=q_hbm.at[:, columns(s, core, QW)],
            dst_ref=qbuf.at[s, other],
            send_sem=snd_q.at[s],
            recv_sem=rem_q.at[s],
            device_id=partner,
            device_id_type=MESH,
        )

    def from_go(s):
        return pltpu.make_async_remote_copy(
            src_ref=go_hbm.at[:, columns(s, core, VW)],
            dst_ref=gobuf.at[s, other],
            send_sem=snd_go.at[s],
            recv_sem=rem_go.at[s],
            device_id=partner,
            device_id_type=MESH,
        )

    def gather_copy(half, dx, dy, piece, axis, sign):
        first, count = rows_of(half, piece)
        there = (dx - sign, dy) if axis == "x" else (dx, dy - sign)
        there = (there[0] % 4, there[1] % 4)
        index = GATHER[(half, there[0], there[1], piece)]
        return pltpu.make_async_remote_copy(
            src_ref=wbuf.at[slot_of(dx, dy), pl.ds(first, count)],
            dst_ref=wbuf.at[slot_of(*there), pl.ds(first, count)],
            send_sem=ag_send.at[index],
            recv_sem=ag_recv.at[index],
            device_id=me.neighbour(axis, sign),
            device_id_type=MESH,
        )

    def gather_wait(half, dx, dy, piece):
        first, count = rows_of(half, piece)
        index = GATHER[(half, dx, dy, piece)]
        pltpu.make_async_remote_copy(
            src_ref=wbuf.at[slot_of(dx, dy), pl.ds(first, count)],
            dst_ref=wbuf.at[slot_of(dx, dy), pl.ds(first, count)],
            send_sem=ag_send.at[index],
            recv_sem=ag_recv.at[index],
            device_id=me.neighbour("x", 1),
            device_id_type=MESH,
        ).wait_recv()

    def gather_event(half, along, across):
        first_axis = main_axis(half)
        second_axis = "y" if first_axis == "x" else "x"
        dx, dy = at(first_axis, along, across)
        if along or across:
            last = across if across else along
            for piece in ("0", "1") if last == 2 else ("f",):
                gather_wait(half, dx, dy, piece)
        if across == 0:
            if along == 0:
                for sign in (1, -1):
                    gather_copy(half, dx, dy, "f", first_axis, sign).start()
            elif along == 3:
                gather_copy(half, dx, dy, "0", first_axis, 1).start()
            elif along == 1:
                gather_copy(half, dx, dy, "1", first_axis, -1).start()
            for sign in (1, -1):
                gather_copy(half, dx, dy, "f", second_axis, sign).start()
        elif across == 3:
            gather_copy(half, dx, dy, "0", second_axis, 1).start()
        elif across == 1:
            gather_copy(half, dx, dy, "1", second_axis, -1).start()

    def gather_sends():
        done = []
        for half in (0, 1):
            first_axis = main_axis(half)
            second_axis = "y" if first_axis == "x" else "x"
            for along in range(4):
                dx, dy = at(first_axis, along, 0)
                if along == 0:
                    done += [(half, dx, dy, "f", first_axis, 1), (half, dx, dy, "f", first_axis, -1)]
                elif along == 3:
                    done += [(half, dx, dy, "0", first_axis, 1)]
                elif along == 1:
                    done += [(half, dx, dy, "1", first_axis, -1)]
                done += [(half, dx, dy, "f", second_axis, 1), (half, dx, dy, "f", second_axis, -1)]
                dx, dy = at(first_axis, along, 3)
                done += [(half, dx, dy, "0", second_axis, 1)]
                dx, dy = at(first_axis, along, 1)
                done += [(half, dx, dy, "1", second_axis, -1)]
        return done

    nearest = [(0, 1, 0), (0, 3, 0), (1, 1, 0), (1, 3, 0)]
    events = {
        0: [(1, 0, 1)],
        1: [(0, 0, 1), (1, 0, 3), (0, 0, 3)],
        2: [(0, 2, 0), (1, 2, 0), (0, 1, 1), (1, 1, 1)],
        3: [(0, 1, 3), (1, 3, 1)],
        4: [(0, 3, 1), (1, 1, 3)],
        5: [(0, 2, 1), (1, 1, 2), (0, 3, 3), (1, 3, 3)],
        6: [(0, 1, 2), (1, 2, 1), (0, 2, 3), (1, 2, 3)],
        7: [(1, 3, 2)],
        8: [(0, 3, 2)],
        9: [(0, 2, 2), (1, 2, 2)],
        10: [(1, 0, 2)],
        11: [(0, 0, 2)],
    }

    def round_copy(source, dest, sems, away):
        to = (me.ctx + away) % 32
        return pltpu.make_async_remote_copy(
            src_ref=source.at[pl.ds(2 * to, 2)],
            dst_ref=dest.at[pl.ds(2 * me.ctx, 2)],
            send_sem=sems[0].at[away],
            recv_sem=sems[1].at[away],
            device_id=ctx_device(away),
            device_id_type=MESH,
        )

    def round_start(source, dest, sems):
        def go(away, carry):
            round_copy(source, dest, sems, away).start()
            return carry

        lax.fori_loop(1, 32, go, 0)
        for t in range(2):
            dest[2 * me.ctx + t] = source[2 * me.ctx + t]

    def round_wait(source, dest, sems):
        def go(away, carry):
            frm = (me.ctx + 32 - away) % 32
            pltpu.make_async_remote_copy(
                src_ref=source.at[pl.ds(2 * frm, 2)],
                dst_ref=dest.at[pl.ds(2 * frm, 2)],
                send_sem=sems[0].at[away],
                recv_sem=sems[1].at[away],
                device_id=ctx_device(away),
                device_id_type=MESH,
            ).wait_recv()
            return carry

        lax.fori_loop(1, 32, go, 0)

    def round_end(source, dest, sems):
        def go(away, carry):
            round_copy(source, dest, sems, away).wait_send()
            return carry

        lax.fori_loop(1, 32, go, 0)

    def cut(read, dest):
        for i in range(4):
            for t in range(2):
                rows = read(t * STRETCH + 16 * i, 16)
                for j in range(8):
                    dest[2 * (8 * i + j) + t, :, :CUT] = rows[:, CUT * j : CUT * (j + 1)]

    def join(source, t, i):
        return jnp.concatenate([source[2 * (8 * i + j) + t, :, :CUT] for j in range(8)], 1)

    hbuf = (hb0, hb1, hb2, hb3, hb4, hb5, hb6, hb7)
    rounds = [(hsem.at[2 * i], hsem.at[2 * i + 1]) for i in range(4)]

    @pl.when(is_source)
    def _():
        wbuf[OWN_SLOT] = w_ref[...]
        gather_event(0, 0, 0)
        gather_event(1, 0, 0)

    latb[core, OWN:, :] = lat_ref[...].T
    cut(lambda first, count: latb[core, OWN + first : OWN + first + count, :], hb0)
    round_start(hb0, hb1, rounds[0])
    lat_copy(core, OWN).start()

    def start_tokens(s, carry):
        away_q(s).start()
        away_go(s).start()
        own_q(s).start()
        own_go(s).start()
        return carry

    lax.fori_loop(0, 16, start_tokens, 0)

    lengths = jnp.broadcast_to(lens_ref[...].astype(F32), (OWN, OWN)).T.astype(BF16)
    down = lax.broadcasted_iota(jnp.int32, (OWN, OWN), 0)
    over = lax.broadcasted_iota(jnp.int32, (OWN, OWN), 1)
    earlier = jnp.where(over < down, 1.0, 0.0).astype(BF16)
    starts = jnp.dot(earlier, lengths, preferred_element_type=F32)
    lane = lax.broadcasted_iota(jnp.int32, (1, OWN), 1)
    first_row = STRETCH * jnp.where(lane < STRETCH, order_ref[0, 2 * me.ctx], order_ref[0, 2 * me.ctx + 1])
    position = (first_row + lane % STRETCH).astype(F32)
    begin = jnp.max(jnp.where(starts <= position, starts, 0.0), 0, keepdims=True)
    klob[core] = jnp.broadcast_to(begin - (first_row - STRETCH).astype(F32), (8, OWN))
    klo_copy(core).start()

    round_wait(hb0, hb1, rounds[0])
    for s in range(64):
        hb2[s] = hb1[jnp.maximum(moves_ref[0, s], 0)]
    round_start(hb2, hb3, rounds[1])

    @pl.when(is_source)
    def _():
        for event in nearest:
            gather_event(*event)

    @pl.when(jnp.logical_not(is_source))
    def _():
        for half in (0, 1):
            z_copy(w_ref, me.zh, me.zl, half).wait_recv()

            @pl.when(at_end)
            def _(half=half):
                z_forward(half).start()

            gather_event(half, 0, 0)

    klo_copy(other).wait_recv()
    key = lax.broadcasted_iota(jnp.int32, (KEYS, OWN), 0)
    row = lax.broadcasted_iota(jnp.int32, (KEYS, OWN), 1)
    spot = (key % STRETCH + STRETCH * (key // OWN)).astype(F32)
    latest = (STRETCH + row % STRETCH).astype(F32)
    same = ((key % OWN) // STRETCH) == (row // STRETCH)
    for trace in range(2):
        allowed = same & (spot <= latest) & (spot >= klob[trace, 0:1, :])
        bias[trace] = jnp.where(allowed, 0.0, -jnp.inf)
    acc[...] = jnp.zeros_like(acc)

    round_wait(hb2, hb3, rounds[1])
    for t in range(2):
        for i in range(4):
            first = t * STRETCH + 16 * i
            latb[core, first : first + 16, :] = join(hb3, t, i)
    lat_copy(core, 0).start()
    lat_copy(other, OWN).wait_recv()
    lat_copy(other, 0).wait_recv()
    for trace in range(2):
        lat_t[:, trace * KEYS : (trace + 1) * KEYS] = latb[trace, :, :D_LAT].T

    def dot(a, b, ca=1, cb=0):
        return lax.dot_general(a, b, (((ca,), (cb,)), ((), ())), preferred_element_type=F32)

    def local_gq(s):
        return pltpu.make_async_copy(gqbuf.at[s, core], gq_hbm.at[:, columns(s, core, QW)], gq_loc.at[s])

    def away_gq(s):
        return pltpu.make_async_remote_copy(
            src_ref=gqbuf.at[s, other],
            dst_ref=gq_hbm.at[:, columns(s, core, QW)],
            send_sem=gq_snd.at[s],
            recv_sem=gq_rcv.at[s],
            device_id=partner,
            device_id_type=MESH,
        )

    def from_gq(s):
        return pltpu.make_async_remote_copy(
            src_ref=gqbuf.at[s, other],
            dst_ref=gq_hbm.at[:, columns(s, other, QW)],
            send_sem=gq_snd.at[s],
            recv_sem=gq_rcv.at[s],
            device_id=partner,
            device_id_type=MESH,
        )

    def reduce_copy(half, phase, across, piece, axis, sign, dx, dy, rows, index_piece):
        first, count = rows
        index, row, _ = REDUCE[(half, phase, across, index_piece)]
        return pltpu.make_async_remote_copy(
            src_ref=gbuf.at[slot_of(dx, dy), pl.ds(first, count)],
            dst_ref=rbuf.at[pl.ds(row, count)],
            send_sem=rs_send.at[index],
            recv_sem=rs_recv.at[index],
            device_id=me.neighbour(axis, sign),
            device_id_type=MESH,
        )

    def reduce_plan(half, phase, across):
        first_axis = main_axis(half)
        second_axis = "y" if first_axis == "x" else "x"
        axis = second_axis if phase == 0 else first_axis

        def place_of(step):
            return at(first_axis, across, step) if phase == 0 else at(first_axis, step, 0)

        far, back, ahead = place_of(2), place_of(3), place_of(1)
        whole = rows_of(half, "f")
        return {
            "0": reduce_copy(half, phase, across, "0", axis, -1, *far, rows_of(half, "0"), "0"),
            "1": reduce_copy(half, phase, across, "1", axis, 1, *far, rows_of(half, "1"), "1"),
            "back": reduce_copy(half, phase, across, "f", axis, -1, *back, whole, "from1"),
            "ahead": reduce_copy(half, phase, across, "f", axis, 1, *ahead, whole, "from3"),
            "slots": (slot_of(*back), slot_of(*ahead), slot_of(*place_of(0))),
        }

    plans = {
        (half, phase, across): reduce_plan(half, phase, across)
        for half in (0, 1)
        for phase in (0, 1)
        for across in (range(4) if phase == 0 else (0,))
    }

    def add_rows(slot, first, count, sources):
        def go(i, carry):
            start = pl.multiple_of(i * 32, 32)
            span = pl.ds(first + start, 32)
            total = gbuf[slot, span, :].astype(F32)
            for source in sources:
                total = total + rbuf[pl.ds(source + start, 32), :].astype(F32)
            gbuf[slot, span, :] = total.astype(BF16)
            return carry

        lax.fori_loop(0, count // 32, go, 0)

    def stage_far(half, phase, across):
        plan = plans[(half, phase, across)]
        plan["0"].start()
        plan["1"].start()

    def stage_near(half, phase, across):
        plan = plans[(half, phase, across)]
        back, ahead, _ = plan["slots"]
        for piece, slot, name in (("0", back, "back"), ("1", ahead, "ahead")):
            plan[piece].wait_recv()
            first, count = rows_of(half, piece)
            add_rows(slot, first, count, [REDUCE[(half, phase, across, piece)][1]])
            plan[name].start()

    def stage_own(half, phase, across):
        plan = plans[(half, phase, across)]
        plan["back"].wait_recv()
        plan["ahead"].wait_recv()
        first, count = rows_of(half, "f")
        own = plan["slots"][2]
        sources = [REDUCE[(half, phase, across, name)][1] for name in ("from1", "from3")]
        add_rows(own, first, count, sources)

    sums = {
        5: [(stage_far, 1, 0, 1)],
        6: [(stage_far, 0, 0, 1)],
        7: [(stage_far, 1, 0, 3), (stage_near, 1, 0, 1)],
        8: [(stage_far, 0, 0, 3), (stage_near, 0, 0, 1)],
        9: [(stage_far, 0, 0, 2), (stage_far, 1, 0, 2), (stage_own, 1, 0, 1)],
        10: [(stage_far, 1, 0, 0), (stage_own, 0, 0, 1)],
        11: [(stage_far, 0, 0, 0), (stage_near, 0, 0, 2), (stage_near, 1, 0, 2)],
        12: [(stage_near, 0, 0, 3), (stage_near, 1, 0, 3)],
        13: [
            (stage_own, 0, 0, 2),
            (stage_far, 0, 1, 0),
            (stage_own, 1, 0, 2),
            (stage_far, 1, 1, 0),
            (stage_near, 1, 0, 0),
        ],
        14: [(stage_near, 0, 0, 0), (stage_own, 0, 0, 3), (stage_own, 1, 0, 3)],
        15: [(stage_near, 0, 1, 0), (stage_near, 1, 1, 0)],
    }

    def step_body(s, carry):
        for at_step, todo in events.items():
            if todo:

                @pl.when(s == at_step)
                def _(todo=todo, at_step=at_step):
                    if at_step == 0:

                        @pl.when(jnp.logical_not(is_source))
                        def _():
                            for event in nearest:
                                gather_event(*event)

                    for event in todo:
                        gather_event(*event)

        own_q(s).wait()
        own_go(s).wait()
        from_q(s).wait_recv()
        from_go(s).wait_recv()
        for trace in range(2):
            kvbuf[trace * KEYS : (trace + 1) * KEYS, :] = dot(latb[trace, :, :D_LAT], wbuf[s]).astype(BF16)
        for trace in range(2):
            span = slice(trace * KEYS, (trace + 1) * KEYS)
            rope = latb[trace, :, D_LAT:]
            queries = qbuf[s, trace]
            grads = gobuf[s, trace]
            out = []
            grope = None
            for head in range(2):
                base = head * (D_NOPE + D_V)
                keys = jnp.concatenate([kvbuf[span, base : base + D_NOPE], rope], 1)
                values = kvbuf[span, base + D_NOPE : base + D_NOPE + D_V]
                query = queries[:, head * (D_NOPE + D_ROPE) : (head + 1) * (D_NOPE + D_ROPE)]
                grad = grads[:, head * D_V : (head + 1) * D_V]
                scores = dot(keys, query, 1, 1) * SCALE + bias[trace]
                highest = jnp.max(scores, 0, keepdims=True)
                expo = jnp.exp(scores - highest)
                probs = expo * (1.0 / jnp.sum(expo, 0, keepdims=True))
                dprob = dot(values, grad, 1, 1)
                delta = jnp.sum(probs * dprob, 0, keepdims=True)
                dscore = (probs * (dprob - delta) * SCALE).astype(BF16)
                gkey = dot(dscore, query)
                gkvbuf[span, base : base + D_NOPE] = gkey[:, :D_NOPE].astype(BF16)
                gkvbuf[span, base + D_NOPE : base + D_NOPE + D_V] = dot(probs.astype(BF16), grad).astype(BF16)
                grope = gkey[:, D_NOPE:] if grope is None else grope + gkey[:, D_NOPE:]
                out.append(dot(dscore, keys, 0, 0).astype(BF16))
            gqbuf[s, trace] = jnp.concatenate(out, 1)
            acc[trace, :, D_LAT:] += grope
        local_gq(s).start()
        away_gq(s).start()
        for trace in range(2):
            acc[trace, :, :D_LAT] += dot(gkvbuf[trace * KEYS : (trace + 1) * KEYS, :], wbuf[s], 1, 1)
        gbuf[s] = dot(lat_t[...], gkvbuf[...]).astype(BF16)
        for at_step, todo in sums.items():

            @pl.when(s == at_step)
            def _(todo=todo):
                for stage, half, phase, across in todo:
                    stage(half, phase, across)

        return carry

    lax.fori_loop(0, 16, step_body, 0)

    acc_away = pltpu.make_async_remote_copy(
        src_ref=acc.at[other], dst_ref=accin, send_sem=misc.at[0], recv_sem=misc.at[1], device_id=partner, device_id_type=MESH
    )
    acc_away.start()

    def z_first(zl):
        return pltpu.make_async_remote_copy(
            src_ref=gbuf.at[OWN_SLOT, pl.ds(zl * QUARTER, QUARTER)],
            dst_ref=parts.at[place],
            send_sem=z_send.at[zl],
            recv_sem=z_recv.at[place],
            device_id=me.device(zh=core, zl=zl),
            device_id_type=MESH,
        )

    def not_mine(zl):
        return jnp.logical_not(jnp.logical_and(is_source, me.zl == zl))

    for half in (0, 1):
        stage_own(half, 0, 0)
        stage_own(half, 1, 0)
        for zl in (2 * half, 2 * half + 1):

            @pl.when(not_mine(zl))
            def _(zl=zl):
                z_first(zl).start()

    acc_away.wait_recv()
    cut(
        lambda first, count: (acc[core, first : first + count, :] + accin[first : first + count, :]).astype(BF16),
        hb4,
    )
    round_start(hb4, hb5, rounds[2])

    round_wait(hb4, hb5, rounds[2])
    for s in range(64):
        moved = hb5[jnp.maximum(moves_ref[1, s], 0)]
        hb6[s] = jnp.where(moves_ref[1, s] >= 0, moved, jnp.zeros_like(moved))
    round_start(hb6, hb7, rounds[3])

    def z_second(zl):
        return pltpu.make_async_remote_copy(
            src_ref=pieces.at[me.zl],
            dst_ref=pieces.at[me.zl],
            send_sem=z_send.at[4 + zl],
            recv_sem=z_recv.at[8 + me.zl],
            device_id=me.device(zl=zl),
            device_id_type=MESH,
        )

    def z_third(zl):
        return pltpu.make_async_remote_copy(
            src_ref=pieces.at[zl],
            dst_ref=pieces.at[zl],
            send_sem=z_send.at[8 + zl],
            recv_sem=z_recv.at[12 + zl],
            device_id=partner,
            device_id_type=MESH,
        )

    @pl.when(is_source)
    def _():
        for source in range(8):

            @pl.when(place != source)
            def _(source=source):
                pltpu.make_async_remote_copy(
                    src_ref=parts.at[source],
                    dst_ref=parts.at[source],
                    send_sem=z_send.at[0],
                    recv_sem=z_recv.at[source],
                    device_id=partner,
                    device_id_type=MESH,
                ).wait_recv()

        parts[place] = gbuf[OWN_SLOT, pl.ds(pl.multiple_of(me.zl * QUARTER, QUARTER), QUARTER), :]

        def total_rows(i, carry):
            span = pl.ds(pl.multiple_of(i * 16, 16), 16)
            total = parts[0, span, :].astype(F32)
            for source in range(1, 8):
                total = total + parts[source, span, :].astype(F32)
            pieces[me.zl, span, :] = total.astype(BF16)
            return carry

        lax.fori_loop(0, QUARTER // 16, total_rows, 0)
        for zl in range(4):

            @pl.when(me.zl != zl)
            def _(zl=zl):
                z_second(zl).start()

        for away in range(4):
            zl = (me.zl + away) % 4
            if away:
                pltpu.make_async_remote_copy(
                    src_ref=pieces.at[zl],
                    dst_ref=pieces.at[zl],
                    send_sem=z_send.at[4],
                    recv_sem=z_recv.at[8 + zl],
                    device_id=partner,
                    device_id_type=MESH,
                ).wait_recv()
            z_third(zl).start()

    round_wait(hb6, hb7, rounds[3])
    for t in range(2):
        for i in range(4):
            first = t * STRETCH + 16 * i
            span = slice(OWN + first, OWN + first + 16)
            accin[span, :] += acc[core, span, :] + join(hb7, t, i).astype(F32)
    glat_ref[...] = accin[OWN:, :].T.astype(BF16)

    @pl.when(jnp.logical_not(is_source))
    def _():
        for zl in range(4):
            z_third(zl).wait_recv()

    for zl in range(4):
        weight_ref[zl * QUARTER : (zl + 1) * QUARTER, :] = pieces[zl].astype(F32)

    def finish(s, carry):
        away_q(s).wait_send()
        away_go(s).wait_send()
        local_gq(s).wait()
        away_gq(s).wait_send()
        from_gq(s).wait_recv()
        return carry

    lax.fori_loop(0, 16, finish, 0)
    acc_away.wait_send()
    lat_copy(core, OWN).wait_send()
    lat_copy(core, 0).wait_send()
    klo_copy(core).wait_send()
    for i in range(4):
        round_end(hbuf[2 * i], hbuf[2 * i + 1], rounds[i])
    for zl in range(4):

        @pl.when(not_mine(zl))
        def _(zl=zl):
            z_first(zl).wait_send()

        @pl.when(jnp.logical_and(is_source, me.zl != zl))
        def _(zl=zl):
            z_second(zl).wait_send()

        @pl.when(is_source)
        def _(zl=zl):
            z_third(zl).wait_send()

    for args in gather_sends():
        gather_copy(*args).wait_send()
    for plan in plans.values():
        for name in ("0", "1", "back", "ahead"):
            plan[name].wait_send()

    @pl.when(z_sends)
    def _():
        for half in (0, 1):
            z_send_copy(half).wait_send()

    @pl.when(z_forwards)
    def _():
        for half in (0, 1):
            z_forward(half).wait_send()


def main_call(queries, grad_out, latent, lengths, order, moves, weight):
    dma = pltpu.SemaphoreType.DMA
    any_spec = pl.BlockSpec(memory_space=pl.ANY)
    vmem = pl.BlockSpec(memory_space=pltpu.VMEM)
    smem = pl.BlockSpec(memory_space=pltpu.SMEM)
    return pl.pallas_call(
        main_kernel,
        out_shape=(
            jax.ShapeDtypeStruct(queries.shape, BF16),
            jax.ShapeDtypeStruct(latent.shape, BF16),
            jax.ShapeDtypeStruct(weight.shape, F32),
        ),
        in_specs=[any_spec, any_spec, vmem, vmem, smem, smem, vmem],
        out_specs=(any_spec, vmem, vmem),
        scratch_shapes=[
            pltpu.VMEM((16, 2, OWN, QW), BF16),
            pltpu.VMEM((16, 2, OWN, VW), BF16),
            pltpu.VMEM((16, 2, OWN, QW), BF16),
            pltpu.VMEM((2, KEYS, D_ALL), BF16),
            pltpu.VMEM((D_LAT, 2 * KEYS), BF16),
            pltpu.VMEM((2, 8, OWN), F32),
            pltpu.VMEM((2, KEYS, OWN), F32),
            pltpu.VMEM((16, D_LAT, KVW), BF16),
            pltpu.VMEM((16, D_LAT, KVW), BF16),
            pltpu.VMEM((REDUCE_ROWS, KVW), BF16),
            pltpu.VMEM((2 * KEYS, KVW), BF16),
            pltpu.VMEM((2 * KEYS, KVW), BF16),
            pltpu.VMEM((2, KEYS, D_ALL), F32),
            pltpu.VMEM((KEYS, D_ALL), F32),
            *[pltpu.VMEM((64, 16, 128), BF16)] * 8,
            pltpu.VMEM((8, QUARTER, KVW), BF16),
            pltpu.VMEM((4, QUARTER, KVW), BF16),
        ]
        + [dma((16,))] * 6
        + [dma((4,)), dma((4,)), dma((8, 32)), dma((12,)), dma((16,)), dma((4,))]
        + [dma((len(GATHER),))] * 2
        + [dma((len(REDUCE),))] * 2
        + [dma((16,))] * 3,
        compiler_params=pltpu.CompilerParams(collective_id=0, has_side_effects=True, vmem_limit_bytes=VMEM_LIMIT),
        cost_estimate=pl.CostEstimate(flops=16_000_000_000, bytes_accessed=12_000_000, transcendentals=2_000_000),
        name="attend",
    )(queries, grad_out, latent, lengths, order, moves, weight)


def per_device(queries, grad_out, latent, up_weight, doc_lengths, stretch_order):
    order = stretch_order[0]
    slots = jnp.arange(order.shape[0], dtype=jnp.int32)
    wanted = order[None, :] + jnp.array([[-1], [1]], jnp.int32)
    moves = jnp.sum(jnp.where(order[None, None, :] == wanted[:, :, None], slots[None, None, :] + 1, 0), 2) - 1
    gq, latent_grad, weight_grad = main_call(
        queries[0], grad_out[0], latent[0].T, doc_lengths, stretch_order, moves, up_weight
    )
    return gq[None], latent_grad.T[None], weight_grad


def solution(mesh):
    in_specs = (
        P("dp", "ctx", None),
        P("dp", "ctx", None),
        P("dp", "ctx", None),
        P(None, "ctx"),
        P("dp", None),
        P("dp", None),
    )
    out_specs = (P("dp", "ctx", None), P("dp", "ctx", None), P(None, "ctx"))
    return jax.shard_map(per_device, mesh=mesh, in_specs=in_specs, out_specs=out_specs, check_vma=False)
```

```python
import jax
import jax.numpy as jnp
from jax import lax
from jax.experimental import pallas as pl
from jax.experimental.pallas import tpu as pltpu
from jax.sharding import PartitionSpec as P


BF16 = jnp.bfloat16
F32 = jnp.float32
MESH = pl.DeviceIdType.MESH

D_NOPE = 128
D_ROPE = 64
D_V = 128
D_LAT = 512
D_ALL = D_LAT + D_ROPE
STRETCH = 64
CUT = D_ALL // 8
OWN = 128
KEYS = 256
QW = 2 * (D_NOPE + D_ROPE)
VW = 2 * D_V
KVW = 2 * (D_NOPE + D_V)
SCALE = (D_NOPE + D_ROPE) ** -0.5
HALF = D_LAT // 2
QUARTER = D_LAT // 4
VMEM_LIMIT = 60 * 1024 * 1024


ORDER = [
    (1, 0), (0, 1), (1, 1), (1, 3), (3, 1), (2, 1), (1, 2), (2, 3),
    (3, 2), (2, 2), (2, 0), (0, 2), (3, 3), (3, 0), (0, 3), (0, 0),
]
OWN_SLOT = ORDER.index((0, 0))


def slot_of(dx, dy):
    return ORDER.index((dx % 4, dy % 4))


def pick(step, digits):
    low = sum(d * 4**i for i, d in enumerate(digits[:8]))
    high = sum(d * 4**i for i, d in enumerate(digits[8:]))
    return lax.shift_right_logical(jnp.where(step < 8, low, high), 2 * (step % 8)) % 4


def rows_of(half, piece):
    base = half * HALF
    if piece == "f":
        return base, HALF
    return base + int(piece) * QUARTER, QUARTER


def main_axis(half):
    return "x" if half == 0 else "y"


def at(axis, along, across):
    return (along, across) if axis == "x" else (across, along)


class Coords:
    def __init__(self):
        dp, ctx = lax.axis_index("dp"), lax.axis_index("ctx")
        self.dp, self.ctx = dp, ctx
        self.zl, self.core = dp // 2, dp % 2
        self.x, self.zh, self.y = ctx // 8, (ctx // 4) % 2, ctx % 4

    def device(self, x=None, y=None, zh=None, zl=None, core=None):
        x = self.x if x is None else x
        y = self.y if y is None else y
        zh = self.zh if zh is None else zh
        zl = self.zl if zl is None else zl
        core = self.core if core is None else core
        return (zl * 2 + core, (x * 2 + zh) * 4 + y)

    def neighbour(self, axis, sign):
        if axis == "x":
            return self.device(x=(self.x + 4 + sign) % 4)
        return self.device(y=(self.y + 4 + sign) % 4)


def gather_keys():
    keys = []
    for half in (0, 1):
        axis = main_axis(half)
        for across in range(4):
            for along in range(4):
                dx, dy = at(axis, along, across)
                if along == 0 and across == 0:
                    continue
                last = across if across else along
                for piece in ("0", "1") if last == 2 else ("f",):
                    keys.append((half, dx, dy, piece))
    return {key: i for i, key in enumerate(keys)}


GATHER = gather_keys()


def reduce_keys():
    keys, row = {}, 0
    for half in (0, 1):
        for across in range(4):
            for phase in (0, 1):
                if phase == 1 and across:
                    continue
                for piece, count in (("0", QUARTER), ("1", QUARTER), ("from1", HALF), ("from3", HALF)):
                    keys[(half, phase, across, piece)] = (len(keys), row, count)
                    row += count
    return keys, row


REDUCE, REDUCE_ROWS = reduce_keys()


def main_kernel(
    q_hbm,
    go_hbm,
    lat_ref,
    lens_ref,
    order_ref,
    moves_ref,
    w_ref,
    gq_hbm,
    glat_ref,
    weight_ref,
    qbuf,
    gobuf,
    gqbuf,
    latb,
    lat_t,
    klob,
    bias,
    wbuf,
    gbuf,
    rbuf,
    kvbuf,
    gkvbuf,
    acc,
    accin,
    hb0,
    hb1,
    hb2,
    hb3,
    hb4,
    hb5,
    hb6,
    hb7,
    moves_in,
    moves,
    parts,
    pieces,
    loc_q,
    loc_go,
    rem_q,
    rem_go,
    snd_q,
    snd_go,
    misc,
    move_sem,
    lat_sem,
    hsem,
    z_send,
    z_recv,
    wz,
    ag_send,
    ag_recv,
    rs_send,
    rs_recv,
    gq_loc,
    gq_snd,
    gq_rcv,
):
    me = Coords()
    core, other = me.core, 1 - me.core
    partner = me.device(core=other)
    is_source = me.zh == core
    at_end = jnp.logical_or(me.zl == 0, me.zl == 3)
    z_sends = jnp.logical_and(is_source, at_end)
    z_forwards = jnp.logical_and(jnp.logical_not(is_source), at_end)
    place = me.zh * 4 + me.zl

    def mover(ctx):
        return (((me.zl + 2) % 4) * 2 + core, ctx)

    barrier = pltpu.get_barrier_semaphore()

    def greet(away, carry):
        pl.semaphore_signal(barrier, inc=1, device_id=mover((me.ctx + away) % 32), device_id_type=MESH)
        return carry

    lax.fori_loop(0, 32, greet, 0)
    for away in (1, 3):
        for zh in (me.zh, 1 - me.zh):
            pl.semaphore_signal(
                barrier, inc=1, device_id=me.device(zh=zh, zl=(me.zl + away) % 4), device_id_type=MESH
            )
    pl.semaphore_signal(barrier, inc=1, device_id=me.device(zh=1 - me.zh), device_id_type=MESH)
    for axis in ("x", "y"):
        for sign in (1, -1):
            pl.semaphore_signal(barrier, inc=1, device_id=me.neighbour(axis, sign), device_id_type=MESH)
    pl.semaphore_signal(barrier, inc=1, device_id=partner, device_id_type=MESH)
    def group_of(step, half):
        dx, dy = pick(step, [d[0] for d in ORDER]), pick(step, [d[1] for d in ORDER])
        return (((me.x + dx) % 4) * 2 + half) * 4 + (me.y + dy) % 4

    def columns(step, half, width):
        return pl.ds(pl.multiple_of(group_of(step, half) * width, width), width)

    def own_q(s):
        return pltpu.make_async_copy(q_hbm.at[:, columns(s, core, QW)], qbuf.at[s, core], loc_q.at[s])

    def own_go(s):
        return pltpu.make_async_copy(go_hbm.at[:, columns(s, core, VW)], gobuf.at[s, core], loc_go.at[s])

    def cut(read, dest):
        for i in range(4):
            for t in range(2):
                rows = read(t * STRETCH + 16 * i, 16)
                for j in range(8):
                    dest[2 * (8 * i + j) + t, :, :CUT] = rows[:, CUT * j : CUT * (j + 1)]

    def start_own(s, carry):
        own_q(s).start()
        own_go(s).start()
        return carry

    lax.fori_loop(0, 16, start_own, 0)
    latb[core, OWN:, :] = lat_ref[...].T
    cut(lambda first, count: latb[core, OWN + first : OWN + first + count, :], hb0)

    lengths = jnp.broadcast_to(lens_ref[...].astype(F32), (OWN, OWN)).T.astype(BF16)
    down = lax.broadcasted_iota(jnp.int32, (OWN, OWN), 0)
    over = lax.broadcasted_iota(jnp.int32, (OWN, OWN), 1)
    earlier = jnp.where(over < down, 1.0, 0.0).astype(BF16)
    starts = jnp.dot(earlier, lengths, preferred_element_type=F32)
    lane = lax.broadcasted_iota(jnp.int32, (1, OWN), 1)
    first_row = STRETCH * jnp.where(lane < STRETCH, order_ref[0, 2 * me.ctx], order_ref[0, 2 * me.ctx + 1])
    position = (first_row + lane % STRETCH).astype(F32)
    begin = jnp.max(jnp.where(starts <= position, starts, 0.0), 0, keepdims=True)
    klob[core] = jnp.broadcast_to(begin - (first_row - STRETCH).astype(F32), (8, OWN))
    acc[...] = jnp.zeros_like(acc)

    @pl.when(is_source)
    def _():
        wbuf[OWN_SLOT] = w_ref[...]

    pl.semaphore_wait(barrier, 42)

    def z_copy(source, zh, zl, half):
        return pltpu.make_async_remote_copy(
            src_ref=source.at[pl.ds(half * HALF, HALF)],
            dst_ref=wbuf.at[OWN_SLOT, pl.ds(half * HALF, HALF)],
            send_sem=wz.at[half],
            recv_sem=wz.at[2 + half],
            device_id=me.device(zh=zh, zl=zl),
            device_id_type=MESH,
        )

    def z_send_copy(half):
        return z_copy(w_ref, 1 - me.zh, jnp.where(me.zl == 3, 0, 3), half)

    def z_forward(half):
        return z_copy(wbuf.at[OWN_SLOT], me.zh, jnp.where(me.zl == 0, 1, 2), half)

    @pl.when(z_sends)
    def _():
        for half in (0, 1):
            z_send_copy(half).start()

    def lat_copy(trace, first):
        index = 2 if first else 0
        return pltpu.make_async_remote_copy(
            src_ref=latb.at[trace, pl.ds(first, OWN)],
            dst_ref=latb.at[trace, pl.ds(first, OWN)],
            send_sem=lat_sem.at[index],
            recv_sem=lat_sem.at[index + 1],
            device_id=partner,
            device_id_type=MESH,
        )

    def klo_copy(trace):
        return pltpu.make_async_remote_copy(
            src_ref=klob.at[trace],
            dst_ref=klob.at[trace],
            send_sem=misc.at[2],
            recv_sem=misc.at[3],
            device_id=partner,
            device_id_type=MESH,
        )

    def away_q(s):
        return pltpu.make_async_remote_copy(
            src_ref=q_hbm.at[:, columns(s, other, QW)],
            dst_ref=qbuf.at[s, core],
            send_sem=snd_q.at[s],
            recv_sem=rem_q.at[s],
            device_id=partner,
            device_id_type=MESH,
        )

    def away_go(s):
        return pltpu.make_async_remote_copy(
            src_ref=go_hbm.at[:, columns(s, other, VW)],
            dst_ref=gobuf.at[s, core],
            send_sem=snd_go.at[s],
            recv_sem=rem_go.at[s],
            device_id=partner,
            device_id_type=MESH,
        )

    def from_q(s):
        return pltpu.make_async_remote_copy(
            src_ref=q_hbm.at[:, columns(s, core, QW)],
            dst_ref=qbuf.at[s, other],
            send_sem=snd_q.at[s],
            recv_sem=rem_q.at[s],
            device_id=partner,
            device_id_type=MESH,
        )

    def from_go(s):
        return pltpu.make_async_remote_copy(
            src_ref=go_hbm.at[:, columns(s, core, VW)],
            dst_ref=gobuf.at[s, other],
            send_sem=snd_go.at[s],
            recv_sem=rem_go.at[s],
            device_id=partner,
            device_id_type=MESH,
        )

    def gather_copy(half, dx, dy, piece, axis, sign):
        first, count = rows_of(half, piece)
        there = (dx - sign, dy) if axis == "x" else (dx, dy - sign)
        there = (there[0] % 4, there[1] % 4)
        index = GATHER[(half, there[0], there[1], piece)]
        return pltpu.make_async_remote_copy(
            src_ref=wbuf.at[slot_of(dx, dy), pl.ds(first, count)],
            dst_ref=wbuf.at[slot_of(*there), pl.ds(first, count)],
            send_sem=ag_send.at[index],
            recv_sem=ag_recv.at[index],
            device_id=me.neighbour(axis, sign),
            device_id_type=MESH,
        )

    def gather_wait(half, dx, dy, piece):
        first, count = rows_of(half, piece)
        index = GATHER[(half, dx, dy, piece)]
        pltpu.make_async_remote_copy(
            src_ref=wbuf.at[slot_of(dx, dy), pl.ds(first, count)],
            dst_ref=wbuf.at[slot_of(dx, dy), pl.ds(first, count)],
            send_sem=ag_send.at[index],
            recv_sem=ag_recv.at[index],
            device_id=me.neighbour("x", 1),
            device_id_type=MESH,
        ).wait_recv()

    def gather_event(half, along, across):
        first_axis = main_axis(half)
        second_axis = "y" if first_axis == "x" else "x"
        dx, dy = at(first_axis, along, across)
        if along or across:
            last = across if across else along
            for piece in ("0", "1") if last == 2 else ("f",):
                gather_wait(half, dx, dy, piece)
        if across == 0:
            if along == 0:
                for sign in (1, -1):
                    gather_copy(half, dx, dy, "f", first_axis, sign).start()
            elif along == 3:
                gather_copy(half, dx, dy, "0", first_axis, 1).start()
            elif along == 1:
                gather_copy(half, dx, dy, "1", first_axis, -1).start()
            for sign in (1, -1):
                gather_copy(half, dx, dy, "f", second_axis, sign).start()
        elif across == 3:
            gather_copy(half, dx, dy, "0", second_axis, 1).start()
        elif across == 1:
            gather_copy(half, dx, dy, "1", second_axis, -1).start()

    def gather_sends():
        done = []
        for half in (0, 1):
            first_axis = main_axis(half)
            second_axis = "y" if first_axis == "x" else "x"
            for along in range(4):
                dx, dy = at(first_axis, along, 0)
                if along == 0:
                    done += [(half, dx, dy, "f", first_axis, 1), (half, dx, dy, "f", first_axis, -1)]
                elif along == 3:
                    done += [(half, dx, dy, "0", first_axis, 1)]
                elif along == 1:
                    done += [(half, dx, dy, "1", first_axis, -1)]
                done += [(half, dx, dy, "f", second_axis, 1), (half, dx, dy, "f", second_axis, -1)]
                dx, dy = at(first_axis, along, 3)
                done += [(half, dx, dy, "0", second_axis, 1)]
                dx, dy = at(first_axis, along, 1)
                done += [(half, dx, dy, "1", second_axis, -1)]
        return done

    nearest = [(0, 1, 0), (0, 3, 0), (1, 1, 0), (1, 3, 0)]
    early = {True: nearest + [(1, 0, 1), (0, 0, 1), (1, 0, 3), (0, 0, 3)], False: []}
    events = {
        0: nearest + [(1, 0, 1)],
        1: [(0, 0, 1), (1, 0, 3), (0, 0, 3)],
        2: [(0, 2, 0), (1, 2, 0), (0, 1, 1), (1, 1, 1)],
        3: [(0, 1, 3), (1, 3, 1)],
        4: [(0, 3, 1), (1, 1, 3)],
        5: [(0, 2, 1), (1, 1, 2), (0, 3, 3), (1, 3, 3)],
        6: [(0, 1, 2), (1, 2, 1), (0, 2, 3), (1, 2, 3)],
        7: [(1, 3, 2)],
        8: [(0, 3, 2)],
        9: [(0, 2, 2), (1, 2, 2)],
        10: [(1, 0, 2)],
        11: [(0, 0, 2)],
    }

    def round_copy(source, dest, sems, to):
        return pltpu.make_async_remote_copy(
            src_ref=source.at[pl.ds(2 * to, 2)],
            dst_ref=dest.at[pl.ds(2 * me.ctx, 2)],
            send_sem=sems[0].at[to],
            recv_sem=sems[1].at[me.ctx],
            device_id=mover(to),
            device_id_type=MESH,
        )

    def round_start(source, dest, sems):
        def go(away, carry):
            round_copy(source, dest, sems, (me.ctx + away) % 32).start()
            return carry

        lax.fori_loop(0, 32, go, 0)

    def round_wait(source, dest, sems):
        def go(frm, carry):
            pltpu.make_async_remote_copy(
                src_ref=source.at[pl.ds(2 * frm, 2)],
                dst_ref=dest.at[pl.ds(2 * frm, 2)],
                send_sem=sems[0].at[frm],
                recv_sem=sems[1].at[frm],
                device_id=mover(frm),
                device_id_type=MESH,
            ).wait_recv()
            return carry

        lax.fori_loop(0, 32, go, 0)

    def round_end(source, dest, sems):
        def go(to, carry):
            round_copy(source, dest, sems, to).wait_send()
            return carry

        lax.fori_loop(0, 32, go, 0)

    moves_away = pltpu.make_async_remote_copy(
        src_ref=moves_ref,
        dst_ref=moves_in,
        send_sem=move_sem.at[0],
        recv_sem=move_sem.at[1],
        device_id=mover(me.ctx),
        device_id_type=MESH,
    )
    moves_here = pltpu.make_async_copy(moves_in, moves, move_sem.at[2])

    def join(source, t, i):
        return jnp.concatenate([source[2 * (8 * i + j) + t, :, :CUT] for j in range(8)], 1)

    hbuf = (hb0, hb1, hb2, hb3, hb4, hb5, hb6, hb7)
    rounds = [(hsem.at[2 * i], hsem.at[2 * i + 1]) for i in range(4)]

    moves_away.start()
    round_start(hb0, hb1, rounds[0])

    @pl.when(is_source)
    def _():
        gather_event(0, 0, 0)
        gather_event(1, 0, 0)

    lat_copy(core, OWN).start()
    klo_copy(core).start()

    def start_tokens(s, carry):
        away_q(s).start()
        away_go(s).start()
        return carry

    lax.fori_loop(0, 16, start_tokens, 0)

    moves_away.wait_recv()
    moves_here.start()
    moves_here.wait()
    round_wait(hb0, hb1, rounds[0])
    for s in range(64):
        hb2[s] = hb1[jnp.maximum(moves[0, s], 0)]
    round_start(hb2, hb3, rounds[1])

    @pl.when(is_source)
    def _():
        for event in early[True]:
            gather_event(*event)

    @pl.when(jnp.logical_not(is_source))
    def _():
        for half in (0, 1):
            z_copy(w_ref, me.zh, me.zl, half).wait_recv()

            @pl.when(at_end)
            def _(half=half):
                z_forward(half).start()

            gather_event(half, 0, 0)

    klo_copy(other).wait_recv()
    key = lax.broadcasted_iota(jnp.int32, (KEYS, OWN), 0)
    row = lax.broadcasted_iota(jnp.int32, (KEYS, OWN), 1)
    spot = (key % STRETCH + STRETCH * (key // OWN)).astype(F32)
    latest = (STRETCH + row % STRETCH).astype(F32)
    same = ((key % OWN) // STRETCH) == (row // STRETCH)
    for trace in range(2):
        allowed = same & (spot <= latest) & (spot >= klob[trace, 0:1, :])
        bias[trace] = jnp.where(allowed, 0.0, -jnp.inf)

    round_wait(hb2, hb3, rounds[1])
    for t in range(2):
        for i in range(4):
            first = t * STRETCH + 16 * i
            latb[core, first : first + 16, :] = join(hb3, t, i)
    lat_copy(core, 0).start()
    lat_copy(other, OWN).wait_recv()
    lat_copy(other, 0).wait_recv()
    for trace in range(2):
        lat_t[:, trace * KEYS : (trace + 1) * KEYS] = latb[trace, :, :D_LAT].T

    def dot(a, b, ca=1, cb=0):
        return lax.dot_general(a, b, (((ca,), (cb,)), ((), ())), preferred_element_type=F32)

    def local_gq(s):
        return pltpu.make_async_copy(gqbuf.at[s, core], gq_hbm.at[:, columns(s, core, QW)], gq_loc.at[s])

    def away_gq(s):
        return pltpu.make_async_remote_copy(
            src_ref=gqbuf.at[s, other],
            dst_ref=gq_hbm.at[:, columns(s, core, QW)],
            send_sem=gq_snd.at[s],
            recv_sem=gq_rcv.at[s],
            device_id=partner,
            device_id_type=MESH,
        )

    def from_gq(s):
        return pltpu.make_async_remote_copy(
            src_ref=gqbuf.at[s, other],
            dst_ref=gq_hbm.at[:, columns(s, other, QW)],
            send_sem=gq_snd.at[s],
            recv_sem=gq_rcv.at[s],
            device_id=partner,
            device_id_type=MESH,
        )

    def reduce_copy(half, phase, across, piece, axis, sign, dx, dy, rows, index_piece):
        first, count = rows
        index, row, _ = REDUCE[(half, phase, across, index_piece)]
        return pltpu.make_async_remote_copy(
            src_ref=gbuf.at[slot_of(dx, dy), pl.ds(first, count)],
            dst_ref=rbuf.at[pl.ds(row, count)],
            send_sem=rs_send.at[index],
            recv_sem=rs_recv.at[index],
            device_id=me.neighbour(axis, sign),
            device_id_type=MESH,
        )

    def reduce_plan(half, phase, across):
        first_axis = main_axis(half)
        second_axis = "y" if first_axis == "x" else "x"
        axis = second_axis if phase == 0 else first_axis

        def place_of(step):
            return at(first_axis, across, step) if phase == 0 else at(first_axis, step, 0)

        far, back, ahead = place_of(2), place_of(3), place_of(1)
        whole = rows_of(half, "f")
        return {
            "0": reduce_copy(half, phase, across, "0", axis, -1, *far, rows_of(half, "0"), "0"),
            "1": reduce_copy(half, phase, across, "1", axis, 1, *far, rows_of(half, "1"), "1"),
            "back": reduce_copy(half, phase, across, "f", axis, -1, *back, whole, "from1"),
            "ahead": reduce_copy(half, phase, across, "f", axis, 1, *ahead, whole, "from3"),
            "slots": (slot_of(*back), slot_of(*ahead), slot_of(*place_of(0))),
        }

    plans = {
        (half, phase, across): reduce_plan(half, phase, across)
        for half in (0, 1)
        for phase in (0, 1)
        for across in (range(4) if phase == 0 else (0,))
    }

    def add_rows(slot, first, count, sources):
        def go(i, carry):
            start = pl.multiple_of(i * 32, 32)
            span = pl.ds(first + start, 32)
            total = gbuf[slot, span, :].astype(F32)
            for source in sources:
                total = total + rbuf[pl.ds(source + start, 32), :].astype(F32)
            gbuf[slot, span, :] = total.astype(BF16)
            return carry

        lax.fori_loop(0, count // 32, go, 0)

    def stage_far(half, phase, across):
        plan = plans[(half, phase, across)]
        plan["0"].start()
        plan["1"].start()

    def stage_near(half, phase, across):
        plan = plans[(half, phase, across)]
        back, ahead, _ = plan["slots"]
        for piece, slot, name in (("0", back, "back"), ("1", ahead, "ahead")):
            plan[piece].wait_recv()
            first, count = rows_of(half, piece)
            add_rows(slot, first, count, [REDUCE[(half, phase, across, piece)][1]])
            plan[name].start()

    def stage_own(half, phase, across):
        plan = plans[(half, phase, across)]
        plan["back"].wait_recv()
        plan["ahead"].wait_recv()
        first, count = rows_of(half, "f")
        own = plan["slots"][2]
        sources = [REDUCE[(half, phase, across, name)][1] for name in ("from1", "from3")]
        add_rows(own, first, count, sources)

    sums = {
        5: [(stage_far, 1, 0, 1)],
        6: [(stage_far, 0, 0, 1)],
        7: [(stage_far, 1, 0, 3), (stage_near, 1, 0, 1)],
        8: [(stage_far, 0, 0, 3), (stage_near, 0, 0, 1)],
        9: [(stage_far, 0, 0, 2), (stage_far, 1, 0, 2), (stage_own, 1, 0, 1)],
        10: [(stage_far, 1, 0, 0), (stage_own, 0, 0, 1)],
        11: [(stage_far, 0, 0, 0), (stage_near, 0, 0, 2), (stage_near, 1, 0, 2)],
        12: [(stage_near, 0, 0, 3), (stage_near, 1, 0, 3)],
        13: [
            (stage_own, 0, 0, 2),
            (stage_far, 0, 1, 0),
            (stage_own, 1, 0, 2),
            (stage_far, 1, 1, 0),
            (stage_near, 1, 0, 0),
        ],
        14: [(stage_near, 0, 0, 0), (stage_own, 0, 0, 3), (stage_own, 1, 0, 3)],
        15: [(stage_near, 0, 1, 0), (stage_near, 1, 1, 0)],
    }

    def step_body(s, carry):
        for at_step, todo in events.items():
            if todo:

                @pl.when(s == at_step)
                def _(todo=todo):
                    for event in todo:
                        if event in early[True] and event in early[False]:
                            continue
                        if event in early[True]:

                            @pl.when(jnp.logical_not(is_source))
                            def _(event=event):
                                gather_event(*event)
                        else:
                            gather_event(*event)

        own_q(s).wait()
        own_go(s).wait()
        from_q(s).wait_recv()
        from_go(s).wait_recv()
        for trace in range(2):
            kvbuf[trace * KEYS : (trace + 1) * KEYS, :] = dot(latb[trace, :, :D_LAT], wbuf[s]).astype(BF16)
        for trace in range(2):
            span = slice(trace * KEYS, (trace + 1) * KEYS)
            rope = latb[trace, :, D_LAT:]
            queries = qbuf[s, trace]
            grads = gobuf[s, trace]
            out = []
            grope = None
            for head in range(2):
                base = head * (D_NOPE + D_V)
                keys = jnp.concatenate([kvbuf[span, base : base + D_NOPE], rope], 1)
                values = kvbuf[span, base + D_NOPE : base + D_NOPE + D_V]
                query = queries[:, head * (D_NOPE + D_ROPE) : (head + 1) * (D_NOPE + D_ROPE)]
                grad = grads[:, head * D_V : (head + 1) * D_V]
                scores = dot(keys, query, 1, 1) * SCALE + bias[trace]
                highest = jnp.max(scores, 0, keepdims=True)
                expo = jnp.exp(scores - highest)
                probs = expo * (1.0 / jnp.sum(expo, 0, keepdims=True))
                dprob = dot(values, grad, 1, 1)
                delta = jnp.sum(probs * dprob, 0, keepdims=True)
                dscore = (probs * (dprob - delta) * SCALE).astype(BF16)
                gkey = dot(dscore, query)
                gkvbuf[span, base : base + D_NOPE] = gkey[:, :D_NOPE].astype(BF16)
                gkvbuf[span, base + D_NOPE : base + D_NOPE + D_V] = dot(probs.astype(BF16), grad).astype(BF16)
                grope = gkey[:, D_NOPE:] if grope is None else grope + gkey[:, D_NOPE:]
                out.append(dot(dscore, keys, 0, 0).astype(BF16))
            gqbuf[s, trace] = jnp.concatenate(out, 1)
            acc[trace, :, D_LAT:] += grope
        local_gq(s).start()
        away_gq(s).start()
        for trace in range(2):
            acc[trace, :, :D_LAT] += dot(gkvbuf[trace * KEYS : (trace + 1) * KEYS, :], wbuf[s], 1, 1)
        gbuf[s] = dot(lat_t[...], gkvbuf[...]).astype(BF16)
        for at_step, todo in sums.items():

            @pl.when(s == at_step)
            def _(todo=todo):
                for stage, half, phase, across in todo:
                    stage(half, phase, across)

        return carry

    lax.fori_loop(0, 16, step_body, 0)

    acc_away = pltpu.make_async_remote_copy(
        src_ref=acc.at[other], dst_ref=accin, send_sem=misc.at[0], recv_sem=misc.at[1], device_id=partner, device_id_type=MESH
    )
    acc_away.start()

    acc_away.wait_recv()
    cut(
        lambda first, count: (acc[core, first : first + count, :] + accin[first : first + count, :]).astype(BF16),
        hb4,
    )
    round_start(hb4, hb5, rounds[2])

    def z_first(zl):
        return pltpu.make_async_remote_copy(
            src_ref=gbuf.at[OWN_SLOT, pl.ds(zl * QUARTER, QUARTER)],
            dst_ref=parts.at[place],
            send_sem=z_send.at[zl],
            recv_sem=z_recv.at[place],
            device_id=me.device(zh=core, zl=zl),
            device_id_type=MESH,
        )

    def not_mine(zl):
        return jnp.logical_not(jnp.logical_and(is_source, me.zl == zl))

    for half in (0, 1):
        stage_own(half, 0, 0)
        stage_own(half, 1, 0)
        for zl in (2 * half, 2 * half + 1):

            @pl.when(not_mine(zl))
            def _(zl=zl):
                z_first(zl).start()

    round_wait(hb4, hb5, rounds[2])
    for s in range(64):
        moved = hb5[jnp.maximum(moves[1, s], 0)]
        hb6[s] = jnp.where(moves[1, s] >= 0, moved, jnp.zeros_like(moved))
    round_start(hb6, hb7, rounds[3])

    def z_second(zl):
        return pltpu.make_async_remote_copy(
            src_ref=pieces.at[me.zl],
            dst_ref=pieces.at[me.zl],
            send_sem=z_send.at[4 + zl],
            recv_sem=z_recv.at[8 + me.zl],
            device_id=me.device(zl=zl),
            device_id_type=MESH,
        )

    def z_third(zl):
        return pltpu.make_async_remote_copy(
            src_ref=pieces.at[zl],
            dst_ref=pieces.at[zl],
            send_sem=z_send.at[8 + zl],
            recv_sem=z_recv.at[12 + zl],
            device_id=partner,
            device_id_type=MESH,
        )

    @pl.when(is_source)
    def _():
        for source in range(8):

            @pl.when(place != source)
            def _(source=source):
                pltpu.make_async_remote_copy(
                    src_ref=parts.at[source],
                    dst_ref=parts.at[source],
                    send_sem=z_send.at[0],
                    recv_sem=z_recv.at[source],
                    device_id=partner,
                    device_id_type=MESH,
                ).wait_recv()

        parts[place] = gbuf[OWN_SLOT, pl.ds(pl.multiple_of(me.zl * QUARTER, QUARTER), QUARTER), :]

        def total_rows(i, carry):
            span = pl.ds(pl.multiple_of(i * 16, 16), 16)
            total = parts[0, span, :].astype(F32)
            for source in range(1, 8):
                total = total + parts[source, span, :].astype(F32)
            pieces[me.zl, span, :] = total.astype(BF16)
            return carry

        lax.fori_loop(0, QUARTER // 16, total_rows, 0)
        for zl in range(4):

            @pl.when(me.zl != zl)
            def _(zl=zl):
                z_second(zl).start()

        for away in range(4):
            zl = (me.zl + away) % 4
            if away:
                pltpu.make_async_remote_copy(
                    src_ref=pieces.at[zl],
                    dst_ref=pieces.at[zl],
                    send_sem=z_send.at[4],
                    recv_sem=z_recv.at[8 + zl],
                    device_id=partner,
                    device_id_type=MESH,
                ).wait_recv()
            z_third(zl).start()

    round_wait(hb6, hb7, rounds[3])
    for t in range(2):
        for i in range(4):
            first = t * STRETCH + 16 * i
            span = slice(OWN + first, OWN + first + 16)
            accin[span, :] += acc[core, span, :] + join(hb7, t, i).astype(F32)
    glat_ref[...] = accin[OWN:, :].T.astype(BF16)

    @pl.when(jnp.logical_not(is_source))
    def _():
        for zl in range(4):
            z_third(zl).wait_recv()

    for zl in range(4):
        weight_ref[zl * QUARTER : (zl + 1) * QUARTER, :] = pieces[zl].astype(F32)

    def finish(s, carry):
        away_q(s).wait_send()
        away_go(s).wait_send()
        local_gq(s).wait()
        away_gq(s).wait_send()
        from_gq(s).wait_recv()
        return carry

    lax.fori_loop(0, 16, finish, 0)
    acc_away.wait_send()
    moves_away.wait_send()
    lat_copy(core, OWN).wait_send()
    lat_copy(core, 0).wait_send()
    klo_copy(core).wait_send()
    for i in range(4):
        round_end(hbuf[2 * i], hbuf[2 * i + 1], rounds[i])
    for zl in range(4):

        @pl.when(not_mine(zl))
        def _(zl=zl):
            z_first(zl).wait_send()

        @pl.when(jnp.logical_and(is_source, me.zl != zl))
        def _(zl=zl):
            z_second(zl).wait_send()

        @pl.when(is_source)
        def _(zl=zl):
            z_third(zl).wait_send()

    for args in gather_sends():
        gather_copy(*args).wait_send()
    for plan in plans.values():
        for name in ("0", "1", "back", "ahead"):
            plan[name].wait_send()

    @pl.when(z_sends)
    def _():
        for half in (0, 1):
            z_send_copy(half).wait_send()

    @pl.when(z_forwards)
    def _():
        for half in (0, 1):
            z_forward(half).wait_send()


def main_call(queries, grad_out, latent, lengths, order, moves, weight):
    dma = pltpu.SemaphoreType.DMA
    any_spec = pl.BlockSpec(memory_space=pl.ANY)
    vmem = pl.BlockSpec(memory_space=pltpu.VMEM)
    smem = pl.BlockSpec(memory_space=pltpu.SMEM)
    return pl.pallas_call(
        main_kernel,
        out_shape=(
            jax.ShapeDtypeStruct(queries.shape, BF16),
            jax.ShapeDtypeStruct(latent.shape, BF16),
            jax.ShapeDtypeStruct(weight.shape, F32),
        ),
        in_specs=[any_spec, any_spec, vmem, vmem, smem, vmem, vmem],
        out_specs=(any_spec, vmem, vmem),
        scratch_shapes=[
            pltpu.VMEM((16, 2, OWN, QW), BF16),
            pltpu.VMEM((16, 2, OWN, VW), BF16),
            pltpu.VMEM((16, 2, OWN, QW), BF16),
            pltpu.VMEM((2, KEYS, D_ALL), BF16),
            pltpu.VMEM((D_LAT, 2 * KEYS), BF16),
            pltpu.VMEM((2, 8, OWN), F32),
            pltpu.VMEM((2, KEYS, OWN), F32),
            pltpu.VMEM((16, D_LAT, KVW), BF16),
            pltpu.VMEM((16, D_LAT, KVW), BF16),
            pltpu.VMEM((REDUCE_ROWS, KVW), BF16),
            pltpu.VMEM((2 * KEYS, KVW), BF16),
            pltpu.VMEM((2 * KEYS, KVW), BF16),
            pltpu.VMEM((2, KEYS, D_ALL), F32),
            pltpu.VMEM((KEYS, D_ALL), F32),
            *[pltpu.VMEM((64, 16, 128), BF16)] * 8,
            pltpu.VMEM((8, 128), jnp.int32),
            pltpu.SMEM((8, 128), jnp.int32),
            pltpu.VMEM((8, QUARTER, KVW), BF16),
            pltpu.VMEM((4, QUARTER, KVW), BF16),
        ]
        + [dma((16,))] * 6
        + [dma((4,)), dma((3,)), dma((4,)), dma((8, 32)), dma((12,)), dma((16,)), dma((4,))]
        + [dma((len(GATHER),))] * 2
        + [dma((len(REDUCE),))] * 2
        + [dma((16,))] * 3,
        compiler_params=pltpu.CompilerParams(collective_id=0, has_side_effects=True, vmem_limit_bytes=VMEM_LIMIT),
        cost_estimate=pl.CostEstimate(flops=16_000_000_000, bytes_accessed=12_000_000, transcendentals=2_000_000),
        name="attend",
    )(queries, grad_out, latent, lengths, order, moves, weight)


def per_device(queries, grad_out, latent, up_weight, doc_lengths, stretch_order):
    order = stretch_order[0]
    slots = jnp.arange(order.shape[0], dtype=jnp.int32)
    wanted = order[None, :] + jnp.array([[-1], [1]], jnp.int32)
    moves = jnp.sum(jnp.where(order[None, None, :] == wanted[:, :, None], slots[None, None, :] + 1, 0), 2) - 1
    moves = jnp.pad(moves, ((0, 6), (0, 64)))
    gq, latent_grad, weight_grad = main_call(
        queries[0], grad_out[0], latent[0].T, doc_lengths, stretch_order, moves, up_weight
    )
    return gq[None], latent_grad.T[None], weight_grad


def solution(mesh):
    in_specs = (
        P("dp", "ctx", None),
        P("dp", "ctx", None),
        P("dp", "ctx", None),
        P(None, "ctx"),
        P("dp", None),
        P("dp", None),
    )
    out_specs = (P("dp", "ctx", None), P("dp", "ctx", None), P(None, "ctx"))
    return jax.shard_map(per_device, mesh=mesh, in_specs=in_specs, out_specs=out_specs, check_vma=False)
```
